128 devices in a mesh: dp: 16 (over y, z_hi, core), ctx: 8 (over z_lo, x).
Axes of the slice: x: 4, y: 4, z: 4 (z_hi: 2, z_lo: 2; z = z_hi * 2 + z_lo), core: 2. Of those that a mesh axis runs over, the one named last changes fastest.
Arguments:
- qkv_in: bfloat16 [16, 4096, 1280], P('dp', 'ctx'), may hold values from -40 to 40
- dest: int32 [16, 4096], P('dp', 'ctx'), may hold values from 0 to 8191, as said below
- lengths: int32 [16, 4], P('dp'), may hold values from 1 to 2048, 4096 in all within a row
- grad_out: bfloat16 [16, 4096, 8192], P('dp', 'ctx'), may hold values from -0.1875 to 0.1875
Outputs:
- attention: bfloat16 [16, 4096, 1024], P('dp', 'ctx')
- grad_proj: float32 [1024, 8192], P(('dp', 'ctx'))
The draws below stay inside these ranges and needn't reach their ends.
Inputs may be any that keep to these rules, and one draw needn't show every extreme that they name: `dest`: within each slot c of the ctx axis, the values over all data groups at positions c * 512 to (c + 1) * 512 - 1 are each number from 0 to the largest value once, and every device's rows go in equal numbers to each data group. Each group's lengths sum to 4096 and the longest is exactly 2048.
All inputs are finite; a program needn't handle non-finite values.
Results may differ from the reference program's by a relative error of at most 0.017.
Values may be sent and summed in bfloat16 or wider, within the bound.
No kernel may reach another device: no remote copies, remote signals or barrier semaphores. Data moves between devices by JAX's collectives and lax.ppermute only.
A program may use at most 128 MiB of HBM per device.

```python
import math
import jax
import jax.numpy as jnp
import numpy as np
from jax import lax

D = 8192
DH = 128
HQ = 8
TOK_DEV = 512
NDOC = 4
SEQ = 4096
TOKENS = 65536
N_DP = 16
N_CTX = 8


def draw_qkv_in(key, part):
    key = jax.random.fold_in(key, 11)
    col_total = (HQ + 2) * DH
    shape = (N_DP, SEQ, col_total)
    values = jnp.clip(jax.random.normal(jax.random.fold_in(key, 1), shape, jnp.float32), -6.0, 6.0)
    return values.astype(jnp.bfloat16)


def draw_dest(key, part):
    key = jax.random.fold_in(key, 23)
    bucket = TOK_DEV // N_DP
    slot_keys = jax.random.split(jax.random.fold_in(key, 1), N_CTX * N_DP)
    slot_perm = jax.vmap(lambda sub_key: jax.random.permutation(sub_key, TOK_DEV))(slot_keys).astype(jnp.int32)
    slot_perm = slot_perm.reshape(N_CTX, N_DP, N_DP, bucket)
    offsets = (jnp.arange(N_DP, dtype=jnp.int32) * TOK_DEV)[None, :, None, None]
    targets = jnp.transpose(slot_perm + offsets, (2, 0, 1, 3)).reshape(N_DP, N_CTX, TOK_DEV)
    row_keys = jax.random.split(jax.random.fold_in(key, 2), N_DP * N_CTX)
    row_perm = jax.vmap(lambda sub_key: jax.random.permutation(sub_key, TOK_DEV))(row_keys).astype(jnp.int32)
    row_perm = row_perm.reshape(N_DP, N_CTX, TOK_DEV)
    shuffled = jnp.take_along_axis(targets, row_perm, axis=2)
    return shuffled.reshape(N_DP, SEQ).astype(jnp.int32)


def block_scale(own_key, extent, cuts, low, top_value):
    loudness = 1.0
    for axis_at, parts in cuts:
        draws = jax.random.uniform(jax.random.fold_in(jax.random.fold_in(own_key, 6), axis_at), (parts,), jnp.float32, low / len(cuts), top_value / len(cuts))
        loudness = loudness * jnp.repeat(jnp.exp(draws), extent[axis_at] // parts).reshape((-1,) + (1,) * (len(extent) - 1 - axis_at))
    return loudness


def profile(amount, total, bound, skew):
    portions = [(1 << 20) // math.isqrt(standing ** skew) + 1 for standing in range(2, amount + 1)]
    surplus, holding = total - bound - (amount - 1), [1] * (amount - 1)
    while surplus > 0:
        movable = [i for i in range(amount - 1) if holding[i] < bound]
        whole, remaining = sum([portions[i] for i in movable]), surplus
        for i in movable:
            extra = min(bound - holding[i], max(1, remaining * portions[i] // whole), surplus)
            holding[i] = holding[i] + extra
            surplus = surplus - extra
    return np.array([bound] + holding)


def ragged(rng, number_of, total, bound, lean):
    if number_of == 2:
        one = jax.random.randint(rng, (), max(1, total - bound), min(bound, total - 1) + 1)
        return jnp.stack([one, total - one])
    tallies = jnp.asarray(profile(number_of, total, bound, lean), jnp.int32)
    couples = (number_of - 1) // 2
    donor, receiver = tallies[1:1 + 2 * couples:2], tallies[2:2 + 2 * couples:2]
    slack = jnp.minimum(donor - 1, bound - receiver)
    moved = jax.random.randint(jax.random.fold_in(rng, 1), (couples,), 0, 1 << 20) % (slack + 1)
    tallies = tallies.at[1:1 + 2 * couples:2].set(donor - moved).at[2:2 + 2 * couples:2].set(receiver + moved)
    return tallies[jax.random.permutation(jax.random.fold_in(rng, 2), number_of)]


def scatter_about(rng, dims, deviation, limit, cuts=(), kind=jnp.bfloat16):
    result = jax.random.normal(rng, dims, jnp.float32) * deviation
    if len(cuts) > 0:
        result = block_scale(rng, dims, cuts, -0.22, 0.18) * result
    return jnp.clip(result, min=-limit, max=limit).astype(kind)


def setup_inputs(seed: int = 0) -> dict:
    key_of = jax.random.split(jax.random.key(seed), 5)
    return {
        "qkv_in": draw_qkv_in(jax.random.fold_in(key_of[4], 71), 0),
        "dest": draw_dest(jax.random.fold_in(key_of[4], 71), 0),
        "lengths": jax.vmap(lambda own: ragged(own, NDOC, SEQ, SEQ // 2, 2))(jax.random.split(key_of[2], N_DP)).reshape((N_DP, NDOC)).astype(jnp.int32),
        "grad_out": scatter_about(key_of[3], (N_DP, SEQ, D), (8 * (1.0 * TOKENS) ** -0.5), 0.1875, ((0, 16), (1, 8))),
    }


score_floor = -1.0e30


def reference(qkv_in, dest, lengths, grad_out):
    col_width = qkv_in.shape[2]
    head_dim = col_width // (HQ + 2)
    query_cols = HQ * head_dim
    slot_base = (jnp.arange(SEQ, dtype=jnp.int32) // TOK_DEV) * TOK_DEV
    owner_group = (dest // TOK_DEV).astype(jnp.int32)
    owner_pos = (slot_base[None, :] + dest % TOK_DEV).astype(jnp.int32)
    owned = jnp.zeros_like(qkv_in).at[owner_group, owner_pos].set(qkv_in)
    starts = (jnp.cumsum(lengths, axis=1) - lengths).astype(jnp.int32)
    positions = jnp.arange(SEQ, dtype=jnp.int32)
    doc_start = jnp.max(jnp.where(starts[:, None, :] <= positions[None, :, None], starts[:, None, :], 0), axis=2).astype(jnp.int32)
    q_block = min(SEQ, 512)
    n_blocks = SEQ // q_block

    def one_block(block_index):
        group_id = block_index // n_blocks
        q_start = (block_index % n_blocks) * q_block
        group_rows = lax.dynamic_index_in_dim(owned, group_id, 0, keepdims=False)
        q_rows = lax.dynamic_slice_in_dim(group_rows, q_start, q_block, 0)[:, :query_cols]
        q_rows = q_rows.astype(jnp.float32).reshape(q_block, HQ, head_dim)
        key_part = group_rows[:, query_cols:query_cols + head_dim].astype(jnp.float32)
        value_part = group_rows[:, query_cols + head_dim:].astype(jnp.float32)
        scores = jnp.einsum('qhd,kd->hqk', q_rows, key_part) * (head_dim ** -0.5)
        group_first = lax.dynamic_index_in_dim(doc_start, group_id, 0, keepdims=False)
        firsts = lax.dynamic_slice_in_dim(group_first, q_start, q_block, 0)
        q_pos = q_start + jnp.arange(q_block, dtype=jnp.int32)
        visible = (positions[None, :] >= firsts[:, None]) & (positions[None, :] <= q_pos[:, None])
        scores = jnp.where(visible[None], scores, score_floor)
        row_max = jnp.max(scores, axis=2, keepdims=True)
        exp_terms = jnp.where(visible[None], jnp.exp(scores - row_max), 0.0)
        row_sum = jnp.sum(exp_terms, axis=2)
        weights = lax.optimization_barrier(exp_terms.astype(jnp.bfloat16)).astype(jnp.float32)
        head_out = jnp.einsum('hqk,kd->qhd', weights, value_part) / jnp.transpose(row_sum)[:, :, None]
        return head_out.reshape(q_block, query_cols).astype(jnp.bfloat16)

    blocks = lax.map(one_block, jnp.arange(N_DP * n_blocks, dtype=jnp.int32))
    attention = blocks.reshape(N_DP, SEQ, query_cols)
    grad_proj = jnp.dot(attention.reshape(N_DP * SEQ, query_cols).T, grad_out.reshape(N_DP * SEQ, grad_out.shape[2]), preferred_element_type=jnp.float32)
    return attention, grad_proj
```

```python
import functools

import jax
import jax.numpy as jnp
import numpy as np
from jax import lax
from jax.experimental import pallas as pl
from jax.experimental.pallas import tpu as pltpu
from jax.sharding import PartitionSpec as P

HQ = 8
DH = 128
ROWS = 512
GROUPS = 16
SLOTS = 8
BACK = 4
TILE = 256
AXES = ("dp", "ctx")
CHIPS = 64
MIB = 1024 * 1024
SCORE_FLOOR = -1e30
EXP_SCALE = float(DH**-0.5 * np.log2(np.e))
WIDTHS = (1408, 1408, 1280)
OFFSETS = (0, 1408, 2816)
HALF = 4096

FLIPS = {
    "xa": (1, 0, 0),
    "xb": (3, 0, 0),
    "ya": (0, 1, 0),
    "yb": (0, 3, 0),
    "za": (0, 0, 1),
    "zb": (0, 0, 3),
}
SET_A = ("xa", "ya", "za")
SET_B = ("xb", "yb", "zb")


def rotate(names, by):
    return names[by:] + names[:by]


ORDERS = (
    tuple(rotate(SET_A, part) + SET_B for part in range(3)),
    tuple(rotate(SET_B, part) + SET_A for part in range(3)),
)


def place_of(index):
    dp, ctx = index // SLOTS, index % SLOTS
    y, z_hi, core = dp // 4, (dp // 2) % 2, dp % 2
    return ctx % 4, y, z_hi * 2 + ctx // 4, core


def index_of(x, y, z, core):
    return (y * 4 + (z // 2) * 2 + core) * SLOTS + (z % 2) * 4 + x


def flip_pairs(flip_of_core):
    pairs = []
    for index in range(2 * CHIPS):
        x, y, z, core = place_of(index)
        fx, fy, fz = FLIPS[flip_of_core[core]]
        pairs.append((index, index_of(x ^ fx, y ^ fy, z ^ fz, core)))
    return pairs


def core_pairs():
    pairs = []
    for index in range(2 * CHIPS):
        x, y, z, core = place_of(index)
        pairs.append((index, index_of(x, y, z, 1 - core)))
    return pairs


def flip_table():
    table = np.zeros((2, 3, CHIPS, 3), np.int32)
    for core in range(2):
        for part in range(3):
            for block in range(CHIPS):
                flips = np.zeros(3, np.int32)
                for level, name in enumerate(ORDERS[core][part]):
                    if (block >> (5 - level)) & 1:
                        flips ^= np.array(FLIPS[name], np.int32)
                table[core, part, block] = flips
    return table


def dot(a, b, contract):
    return lax.dot_general(
        a, b, ((contract[:1], contract[1:]), ((), ())), preferred_element_type=jnp.float32
    )


def as_bf16(mask):
    return mask.astype(jnp.float32).astype(jnp.bfloat16)


def vmem_call(body, out_shape, scratch=(), smem=0, operands=(), mib=56, flops=0, nbytes=0):
    specs = [pl.BlockSpec(memory_space=pltpu.SMEM)] * smem
    specs += [pl.BlockSpec(memory_space=pltpu.VMEM)] * (len(operands) - smem)
    out_specs = jax.tree.map(lambda _: pl.BlockSpec(memory_space=pltpu.VMEM), out_shape)
    return pl.pallas_call(
        body,
        out_shape=out_shape,
        in_specs=specs,
        out_specs=out_specs,
        scratch_shapes=list(scratch),
        compiler_params=pltpu.CompilerParams(vmem_limit_bytes=mib * MIB),
        cost_estimate=pl.CostEstimate(flops=flops, bytes_accessed=nbytes, transcendentals=0),
    )(*operands)


def sort_kernel(dest_ref, rows_ref, key_vals_ref, queries_ref):
    dest = dest_ref[...]
    target = dest >> 9
    slot = dest & (ROWS - 1)
    member = as_bf16(lax.broadcasted_iota(jnp.int32, (GROUPS, ROWS), 0) == target)
    same = dot(member, member, (0, 0))
    row = lax.broadcasted_iota(jnp.int32, (ROWS, ROWS), 0)
    col = lax.broadcasted_iota(jnp.int32, (ROWS, ROWS), 1)
    rank = jnp.sum(jnp.where(row < col, same, 0.0), axis=0, keepdims=True)
    place = target * (ROWS // GROUPS) + rank.astype(jnp.int32)
    order = as_bf16(row == place)
    line = lax.broadcasted_iota(jnp.int32, (DH, ROWS), 0)
    coded = jnp.where(line == 0, slot >> 4, jnp.where(line == 1, slot & 15, 0))
    coded = coded.astype(jnp.float32).astype(jnp.bfloat16)
    key_vals_ref[:, 2 * DH :] = dot(order, coded, (1, 1)).astype(jnp.bfloat16)
    key_vals_ref[:, : 2 * DH] = dot(order, rows_ref[:, HQ * DH :], (1, 0)).astype(jnp.bfloat16)
    queries_ref[...] = dot(order, rows_ref[:, : HQ * DH], (1, 0)).astype(jnp.bfloat16)


def place_kernel(got_ref, key_vals_ref, inverse_ref):
    lane = lax.broadcasted_iota(jnp.int32, (16, DH), 1)
    coef = jnp.where(lane == 0, 16.0, jnp.where(lane == 1, 1.0, 0.0)).astype(jnp.bfloat16)
    slots = dot(coef, got_ref[:, 2 * DH :], (1, 1))[:1].astype(jnp.int32)
    inverse = as_bf16(lax.broadcasted_iota(jnp.int32, (ROWS, ROWS), 0) == slots)
    inverse_ref[...] = inverse
    key_vals_ref[...] = dot(inverse, got_ref[:, : 2 * DH], (1, 0)).astype(jnp.bfloat16)


def attend_kernel(
    slot_ref,
    lengths_ref,
    inverse_ref,
    got_ref,
    kv0_ref,
    kv1_ref,
    kv2_ref,
    kv3_ref,
    kv4_ref,
    out_ref,
    out_t_ref,
    q_ref,
    k_ref,
    v_ref,
    max_ref,
    sum_ref,
    acc_ref,
):
    for back, kv_ref in enumerate((kv0_ref, kv1_ref, kv2_ref, kv3_ref, kv4_ref)):
        at = (BACK - back) * ROWS
        k_ref[at : at + ROWS, :] = kv_ref[:, :DH]
        v_ref[:, at : at + ROWS] = kv_ref[:, DH:].T
    for h in range(HQ):
        cols = slice(h * DH, (h + 1) * DH)
        placed = dot(inverse_ref[...], got_ref[:, cols], (1, 0)).astype(jnp.bfloat16)
        q_ref[cols, :] = placed.T

    slot = slot_ref[0]
    start1 = lengths_ref[0, 0]
    start2 = start1 + lengths_ref[0, 1]
    start3 = start2 + lengths_ref[0, 2]

    def first_of(position):
        found = jnp.where(position >= start1, start1, 0)
        found = jnp.where(position >= start2, start2, found)
        return jnp.where(position >= start3, start3, found)

    for tile in range(ROWS // TILE):
        q_cols = slice(tile * TILE, (tile + 1) * TILE)
        p_first = slot * ROWS + tile * TILE
        low_first = first_of(p_first)
        high_first = first_of(p_first + TILE - 1)
        q_pos = p_first + lax.broadcasted_iota(jnp.int32, (1, TILE), 1)
        doc_first = first_of(q_pos)
        own_at = BACK * ROWS + tile * TILE

        def block(j, masked, causal, first, q_cols=q_cols, p_first=p_first, own_at=own_at, q_pos=q_pos, doc_first=doc_first):
            if isinstance(j, int):
                at = own_at - j * TILE
            else:
                at = pl.multiple_of(own_at - j * TILE, TILE)
            keys = k_ref[pl.ds(at, TILE), :]
            values = v_ref[:, pl.ds(at, TILE)]
            if masked:
                k_pos = p_first - j * TILE + lax.broadcasted_iota(jnp.int32, (TILE, TILE), 0)
                visible = k_pos >= doc_first
                if causal:
                    visible = visible & (k_pos <= q_pos)
            for h in range(HQ):
                scores = dot(keys, q_ref[h * DH : (h + 1) * DH, q_cols], (1, 0))
                if masked:
                    scores = jnp.where(visible, scores, SCORE_FLOOR)
                top = jnp.max(scores, axis=0, keepdims=True) * EXP_SCALE
                if not first:
                    old = max_ref[h : h + 1, :]
                    top = jnp.maximum(old, top)
                    rescale = jnp.exp2(old - top)
                weights = jnp.exp2(scores * EXP_SCALE - top)
                total = jnp.sum(weights, axis=0, keepdims=True)
                term = dot(values, weights.astype(jnp.bfloat16), (1, 0))
                max_ref[h : h + 1, :] = top
                if first:
                    sum_ref[h : h + 1, :] = total
                    acc_ref[h * DH : (h + 1) * DH, :] = term
                else:
                    sum_ref[h : h + 1, :] = sum_ref[h : h + 1, :] * rescale + total
                    acc_ref[h * DH : (h + 1) * DH, :] = (
                        acc_ref[h * DH : (h + 1) * DH, :] * rescale + term
                    )

        block(0, True, True, True)
        count = (p_first - low_first + TILE - 1) // TILE
        clear = jnp.maximum(p_first - high_first, 0) // TILE

        @pl.loop(1, 1 + clear)
        def _(j):
            block(j, False, False, False)

        @pl.loop(1 + clear, 1 + count)
        def _(j):
            block(j, True, False, False)

        for h in range(HQ):
            rows = slice(h * DH, (h + 1) * DH)
            done = (acc_ref[rows, :] / sum_ref[h : h + 1, :]).astype(jnp.bfloat16)
            out_t_ref[rows, q_cols] = done
            out_ref[q_cols, rows] = done.T


def order_kernel(table_ref, own_ref, other_ref, *refs):
    outs, (own32_ref, other32_ref) = refs[:6], refs[6:]
    own32_ref[...] = own_ref[...].astype(jnp.float32)
    other32_ref[...] = other_ref[...].astype(jnp.float32)
    for part in range(3):
        for half in range(2):
            out_ref = outs[part * 2 + half]

            @pl.loop(0, CHIPS // 2)
            def _(block, part=part, half=half, out_ref=out_ref):
                at = pl.multiple_of(table_ref[part, half * (CHIPS // 2) + block], 8)
                to = pl.ds(pl.multiple_of(block * 16, 16), 16)
                for side, src_ref in enumerate((own32_ref, other32_ref)):
                    both = jnp.concatenate(
                        [src_ref[pl.ds(at, 8), :], src_ref[pl.ds(at + 64, 8), :]], axis=0
                    )
                    out_ref[to, side * ROWS : (side + 1) * ROWS] = both.astype(jnp.bfloat16)


def project_kernel(left_ref, own_ref, other_ref, out_ref):
    for at in range(0, left_ref.shape[0], 256):
        rows = slice(at, at + 256)
        term = dot(left_ref[rows, :ROWS], own_ref[...], (1, 0))
        term += dot(left_ref[rows, ROWS:], other_ref[...], (1, 0))
        out_ref[rows, :] = term.astype(out_ref.dtype)


def shape(rows, cols, dtype=jnp.bfloat16):
    return jax.ShapeDtypeStruct((rows, cols), dtype)


def body(qkv_in, dest, lengths, grad_out):
    dp_at = lax.axis_index("dp")
    slot = lax.axis_index("ctx")
    core = dp_at % 2
    x, y, z = slot % 4, dp_at // 4, ((dp_at // 2) % 2) * 2 + slot // 4
    swap = core_pairs()

    tokens = grad_out[0]
    own_cols = [
        lax.dynamic_slice(tokens, (0, core * HALF + at), (ROWS, width))
        for at, width in zip(OFFSETS, WIDTHS)
    ]
    other_cols = [
        lax.ppermute(
            lax.dynamic_slice(tokens, (0, (1 - core) * HALF + at), (ROWS, width)), AXES, swap
        )
        for at, width in zip(OFFSETS, WIDTHS)
    ]

    sent_kv, sent_q = vmem_call(
        sort_kernel,
        (shape(ROWS, 3 * DH), shape(ROWS, HQ * DH)),
        operands=(dest, qkv_in[0]),
        flops=10**9,
        nbytes=3 * MIB,
    )
    got_kv = lax.all_to_all(
        sent_kv.reshape(GROUPS, ROWS // GROUPS, 3 * DH), "dp", 0, 0, tiled=True
    ).reshape(ROWS, 3 * DH)
    got_q = lax.all_to_all(
        sent_q.reshape(GROUPS, ROWS // GROUPS, HQ * DH), "dp", 0, 0, tiled=True
    ).reshape(ROWS, HQ * DH)
    key_vals, inverse = vmem_call(
        place_kernel,
        (shape(ROWS, 2 * DH), shape(ROWS, ROWS)),
        operands=(got_kv,),
        flops=2 * 10**8,
        nbytes=MIB,
    )
    earlier = [
        lax.ppermute(key_vals, "ctx", [(at, at + back) for at in range(SLOTS - back)])
        for back in range(1, BACK + 1)
    ]

    attention, attention_t = vmem_call(
        attend_kernel,
        (shape(ROWS, HQ * DH), shape(HQ * DH, ROWS)),
        scratch=(
            pltpu.VMEM((HQ * DH, ROWS), jnp.bfloat16),
            pltpu.VMEM(((BACK + 1) * ROWS, DH), jnp.bfloat16),
            pltpu.VMEM((DH, (BACK + 1) * ROWS), jnp.bfloat16),
            pltpu.VMEM((HQ, TILE), jnp.float32),
            pltpu.VMEM((HQ, TILE), jnp.float32),
            pltpu.VMEM((HQ * DH, TILE), jnp.float32),
        ),
        smem=2,
        operands=(slot.reshape(1), lengths, inverse, got_q, key_vals, *earlier),
        flops=10**10,
        nbytes=6 * MIB,
    )
    other_t = lax.ppermute(attention_t, AXES, swap)

    flips = jnp.asarray(flip_table())[core]
    to_x, to_y, to_z = x ^ flips[..., 0], y ^ flips[..., 1], z ^ flips[..., 2]
    table = ((to_y * 2 + to_z // 2) * 128 + ((to_z % 2) * 4 + to_x) * 8).astype(jnp.int32)
    lefts = vmem_call(
        order_kernel,
        tuple(shape(512, 2 * ROWS) for _ in range(6)),
        scratch=(pltpu.VMEM((1024, ROWS), jnp.float32), pltpu.VMEM((1024, ROWS), jnp.float32)),
        smem=1,
        operands=(table, attention_t, other_t),
        flops=10**7,
        nbytes=8 * MIB,
    )

    def project(part, half):
        return vmem_call(
            project_kernel,
            shape(512, WIDTHS[part]),
            operands=(lefts[part * 2 + half], own_cols[part], other_cols[part]),
            flops=2 * 512 * 1024 * WIDTHS[part],
            nbytes=5 * MIB,
        )

    sends = [project(part, 1) for part in range(3)]
    coming = [
        lax.ppermute(sends[part], AXES, flip_pairs([ORDERS[c][part][0] for c in range(2)]))
        for part in range(3)
    ]
    keeps = [project(part, 0) for part in range(3)]
    for level in range(1, 4):
        sums = [
            keep.astype(jnp.float32) + came.astype(jnp.float32)
            for keep, came in zip(keeps, coming)
        ]
        rows = sums[0].shape[0] // 2
        keeps = [total[:rows] for total in sums]
        sends = [total[rows:].astype(jnp.bfloat16) for total in sums]
        if level < 3:
            coming = [
                lax.ppermute(
                    sends[part], AXES, flip_pairs([ORDERS[c][part][level] for c in range(2)])
                )
                for part in range(3)
            ]
    keep, send = jnp.concatenate(keeps, axis=1), jnp.concatenate(sends, axis=1)
    for level in range(3, 6):
        came = lax.ppermute(send, AXES, flip_pairs([ORDERS[c][0][level] for c in range(2)]))
        total = keep + came.astype(jnp.float32)
        rows = total.shape[0] // 2
        keep, send = total[:rows], total[rows:].astype(jnp.bfloat16)
    both = total.reshape(2, 8, HALF)
    mine = lax.dynamic_index_in_dim(both, core, 0, keepdims=False)
    theirs = lax.dynamic_index_in_dim(both, 1 - core, 0, keepdims=False).astype(jnp.bfloat16)
    came = lax.ppermute(theirs, AXES, swap).astype(jnp.float32)
    grad_proj = jnp.where(
        core == 0,
        jnp.concatenate([mine, came], axis=1),
        jnp.concatenate([came, mine], axis=1),
    )
    return attention[None], grad_proj


def solution(mesh):
    in_specs = (P("dp", "ctx", None), P("dp", "ctx"), P("dp", None), P("dp", "ctx", None))
    out_specs = (P("dp", "ctx", None), P(("dp", "ctx"), None))
    return jax.shard_map(body, mesh=mesh, in_specs=in_specs, out_specs=out_specs, check_vma=False)
```

```python
import functools

import jax
import jax.numpy as jnp
import numpy as np
from jax import lax
from jax.experimental import pallas as pl
from jax.experimental.pallas import tpu as pltpu
from jax.sharding import PartitionSpec as P

HQ = 8
DH = 128
ROWS = 512
GROUPS = 16
SLOTS = 8
BACK = 4
TILE = 256
AXES = ("dp", "ctx")
CHIPS = 64
MIB = 1024 * 1024
SCORE_FLOOR = -1e30
TOTAL_LIMIT = 2.0**90
EXP_SCALE = float(DH**-0.5 * np.log2(np.e))
WIDTHS = (1408, 1408, 1280)
OFFSETS = (0, 1408, 2816)
HALF = 4096

FLIPS = {
    "xa": (1, 0, 0),
    "xb": (3, 0, 0),
    "ya": (0, 1, 0),
    "yb": (0, 3, 0),
    "za": (0, 0, 1),
    "zb": (0, 0, 3),
}
SET_A = ("xa", "ya", "za")
SET_B = ("xb", "yb", "zb")


def rotate(names, by):
    return names[by:] + names[:by]


ORDERS = (
    tuple(rotate(SET_A, part) + SET_B for part in range(3)),
    tuple(rotate(SET_B, part) + SET_A for part in range(3)),
)


def place_of(index):
    dp, ctx = index // SLOTS, index % SLOTS
    y, z_hi, core = dp // 4, (dp // 2) % 2, dp % 2
    return ctx % 4, y, z_hi * 2 + ctx // 4, core


def index_of(x, y, z, core):
    return (y * 4 + (z // 2) * 2 + core) * SLOTS + (z % 2) * 4 + x


def flip_pairs(flip_of_core):
    pairs = []
    for index in range(2 * CHIPS):
        x, y, z, core = place_of(index)
        fx, fy, fz = FLIPS[flip_of_core[core]]
        pairs.append((index, index_of(x ^ fx, y ^ fy, z ^ fz, core)))
    return pairs


def core_pairs():
    pairs = []
    for index in range(2 * CHIPS):
        x, y, z, core = place_of(index)
        pairs.append((index, index_of(x, y, z, 1 - core)))
    return pairs


def flip_table():
    table = np.zeros((2, CHIPS, 3), np.int32)
    for core in range(2):
        for block in range(CHIPS):
            for level, name in enumerate(ORDERS[core][0]):
                if (block >> (5 - level)) & 1:
                    table[core, block] ^= np.array(FLIPS[name], np.int32)
    return table


def dot(a, b, contract):
    return lax.dot_general(
        a, b, ((contract[:1], contract[1:]), ((), ())), preferred_element_type=jnp.float32
    )


def as_bf16(mask):
    return mask.astype(jnp.float32).astype(jnp.bfloat16)


def vmem_call(body, out_shape, scratch=(), smem=0, operands=(), mib=16, flops=0, nbytes=0):
    specs = [pl.BlockSpec(memory_space=pltpu.SMEM)] * smem
    specs += [pl.BlockSpec(memory_space=pltpu.VMEM)] * (len(operands) - smem)
    out_specs = jax.tree.map(lambda _: pl.BlockSpec(memory_space=pltpu.VMEM), out_shape)
    return pl.pallas_call(
        body,
        out_shape=out_shape,
        in_specs=specs,
        out_specs=out_specs,
        scratch_shapes=list(scratch),
        compiler_params=pltpu.CompilerParams(vmem_limit_bytes=mib * MIB),
        cost_estimate=pl.CostEstimate(flops=flops, bytes_accessed=nbytes, transcendentals=0),
    )(*operands)


def sort_kernel(dest_ref, rows_ref, key_vals_ref, queries_ref):
    dest = dest_ref[...]
    target = dest >> 9
    slot = dest & (ROWS - 1)
    member = as_bf16(lax.broadcasted_iota(jnp.int32, (GROUPS, ROWS), 0) == target)
    same = dot(member, member, (0, 0))
    row = lax.broadcasted_iota(jnp.int32, (ROWS, ROWS), 0)
    col = lax.broadcasted_iota(jnp.int32, (ROWS, ROWS), 1)
    rank = jnp.sum(jnp.where(row < col, same, 0.0), axis=0, keepdims=True)
    place = target * (ROWS // GROUPS) + rank.astype(jnp.int32)
    order = as_bf16(row == place)
    line = lax.broadcasted_iota(jnp.int32, (DH, ROWS), 0)
    coded = jnp.where(line == 0, slot >> 4, jnp.where(line == 1, slot & 15, 0))
    coded = coded.astype(jnp.float32).astype(jnp.bfloat16)
    key_vals_ref[:, 2 * DH :] = dot(order, coded, (1, 1)).astype(jnp.bfloat16)
    key_vals_ref[:, : 2 * DH] = dot(order, rows_ref[:, HQ * DH :], (1, 0)).astype(jnp.bfloat16)
    queries_ref[...] = dot(order, rows_ref[:, : HQ * DH], (1, 0)).astype(jnp.bfloat16)


def place_kernel(got_ref, key_vals_ref, inverse_ref):
    lane = lax.broadcasted_iota(jnp.int32, (16, DH), 1)
    coef = jnp.where(lane == 0, 16.0, jnp.where(lane == 1, 1.0, 0.0)).astype(jnp.bfloat16)
    slots = dot(coef, got_ref[:, 2 * DH :], (1, 1))[:1].astype(jnp.int32)
    inverse = as_bf16(lax.broadcasted_iota(jnp.int32, (ROWS, ROWS), 0) == slots)
    inverse_ref[...] = inverse
    key_vals_ref[...] = dot(inverse, got_ref[:, : 2 * DH], (1, 0)).astype(jnp.bfloat16)


def attend_kernel(
    slot_ref,
    lengths_ref,
    table_ref,
    inverse_ref,
    got_ref,
    kv0_ref,
    kv1_ref,
    kv2_ref,
    kv3_ref,
    kv4_ref,
    out_ref,
    own_ref,
    swap_ref,
    q_ref,
    k_ref,
    v_ref,
    top_ref,
    acc_ref,
    done_ref,
):
    for back, kv_ref in enumerate((kv0_ref, kv1_ref, kv2_ref, kv3_ref, kv4_ref)):
        at = (BACK - back) * ROWS
        k_ref[at : at + ROWS, :] = kv_ref[:, :DH]
        v_ref[at : at + ROWS, :DH] = kv_ref[:, DH:]
    v_ref[:, DH:] = jnp.ones(((BACK + 1) * ROWS, DH), jnp.bfloat16)
    q_ref[...] = dot(inverse_ref[...], got_ref[...], (1, 0)).astype(jnp.bfloat16)

    slot = slot_ref[0]
    start1 = lengths_ref[0, 0]
    start2 = start1 + lengths_ref[0, 1]
    start3 = start2 + lengths_ref[0, 2]

    def first_of(position):
        found = jnp.where(position >= start1, start1, 0)
        found = jnp.where(position >= start2, start2, found)
        return jnp.where(position >= start3, start3, found)

    for tile in range(ROWS // TILE):
        q_rows = slice(tile * TILE, (tile + 1) * TILE)
        p_first = slot * ROWS + tile * TILE
        low_first = first_of(p_first)
        high_first = first_of(p_first + TILE - 1)
        own_at = BACK * ROWS + tile * TILE
        count = (p_first - low_first + TILE - 1) // TILE
        clear = jnp.maximum(p_first - high_first, 0) // TILE

        def parts(j, p_first=p_first, own_at=own_at):
            at = pl.multiple_of(own_at - j * TILE, TILE)
            return k_ref[pl.ds(at, TILE), :], v_ref[pl.ds(at, TILE), :]

        def visible_of(j, p_first=p_first):
            q_pos = p_first + lax.broadcasted_iota(jnp.int32, (TILE, TILE), 0)
            k_pos = p_first - j * TILE + lax.broadcasted_iota(jnp.int32, (TILE, TILE), 1)
            return (k_pos >= first_of(q_pos)) & (k_pos <= q_pos)

        def scores_of(h, keys, visible, q_rows=q_rows):
            scores = dot(q_ref[q_rows, h * DH : (h + 1) * DH], keys, (1, 1))
            return scores if visible is None else jnp.where(visible, scores, SCORE_FLOOR)

        own_keys = k_ref[own_at : own_at + TILE, :].astype(jnp.float32)
        ones = jnp.ones((DH, DH), jnp.bfloat16)
        for h in range(HQ):
            pair = q_ref[q_rows, h * DH : (h + 1) * DH].astype(jnp.float32) * own_keys
            top_ref[h * TILE : (h + 1) * TILE, :] = (
                dot(pair.astype(jnp.bfloat16), ones, (1, 0)) * EXP_SCALE
            )
        acc_ref[...] = jnp.zeros_like(acc_ref)

        def add(j, masked):
            keys, values = parts(j)
            visible = visible_of(j) if masked else None
            for h in range(HQ):
                rows = slice(h * TILE, (h + 1) * TILE)
                scores = scores_of(h, keys, visible)
                top = top_ref[rows, :]
                top = jnp.concatenate([top, top], axis=1)
                weights = jnp.exp2(scores * EXP_SCALE - top).astype(jnp.bfloat16)
                acc_ref[rows, :] += dot(weights, values, (1, 0))

        add(0, True)

        @pl.loop(1, 1 + clear)
        def _(j):
            add(j, False)

        @pl.loop(1 + clear, 1 + count)
        def _(j):
            add(j, True)

        @pl.when(jnp.max(acc_ref[:, DH:]) > TOTAL_LIMIT)
        def _():
            top_ref[...] = jnp.full_like(top_ref, SCORE_FLOOR)
            acc_ref[...] = jnp.zeros_like(acc_ref)

            @pl.loop(0, 1 + count)
            def _(j):
                keys, values = parts(j)
                visible = visible_of(j)

                @pl.loop(0, HQ)
                def _(h):
                    rows = pl.ds(pl.multiple_of(h * TILE, TILE), TILE)
                    cols = pl.ds(pl.multiple_of(h * DH, DH), DH)
                    scores = dot(q_ref[q_rows, cols], keys, (1, 1))
                    scores = jnp.where(visible, scores, SCORE_FLOOR)
                    old = top_ref[rows, :]
                    best = jnp.max(scores, axis=1, keepdims=True) * EXP_SCALE
                    top = jnp.maximum(old, best)
                    rescale = jnp.exp2(old - top)
                    top_ref[rows, :] = top
                    top = jnp.concatenate([top, top], axis=1)
                    weights = jnp.exp2(scores * EXP_SCALE - top).astype(jnp.bfloat16)
                    rescale = jnp.concatenate([rescale, rescale], axis=1)
                    acc_ref[rows, :] = acc_ref[rows, :] * rescale + dot(weights, values, (1, 0))

        for h in range(HQ):
            rows = slice(h * TILE, (h + 1) * TILE)
            done = acc_ref[rows, :DH] / acc_ref[rows, DH:]
            out_ref[q_rows, h * DH : (h + 1) * DH] = done.astype(jnp.bfloat16)
            done_ref[h * DH : (h + 1) * DH, q_rows] = done.T

    for side, ordered_ref in enumerate((own_ref, swap_ref)):

        @pl.loop(0, CHIPS, unroll=4)
        def _(block, side=side, ordered_ref=ordered_ref):
            at = pl.multiple_of(table_ref[side, block], 8)
            both = jnp.concatenate(
                [done_ref[pl.ds(at, 8), :], done_ref[pl.ds(at + 64, 8), :]], axis=0
            )
            ordered_ref[pl.ds(pl.multiple_of(block * 16, 16), 16), :] = both.astype(jnp.bfloat16)


def project_kernel(level, half, left_ref, left2_ref, own_ref, other_ref, out_ref):
    run = 512 >> level
    step = min(run, 256)
    for at in range(0, 512, step):
        rows = slice(at, at + step)
        source = (at // run) * 2 * run + half * run + at % run
        source = slice(source, source + step)
        term = dot(left_ref[source, :], own_ref[...], (1, 0))
        term += dot(left2_ref[source, :], other_ref[...], (1, 0))
        out_ref[rows, :] = term.astype(out_ref.dtype)


def shape(rows, cols, dtype=jnp.bfloat16):
    return jax.ShapeDtypeStruct((rows, cols), dtype)


def body(qkv_in, dest, lengths, grad_out):
    dp_at = lax.axis_index("dp")
    slot = lax.axis_index("ctx")
    core = dp_at % 2
    x, y, z = slot % 4, dp_at // 4, ((dp_at // 2) % 2) * 2 + slot // 4
    swap = core_pairs()

    tokens = grad_out[0]
    own_cols = [
        lax.dynamic_slice(tokens, (0, core * HALF + at), (ROWS, width))
        for at, width in zip(OFFSETS, WIDTHS)
    ]
    other_cols = [
        lax.ppermute(
            lax.dynamic_slice(tokens, (0, (1 - core) * HALF + at), (ROWS, width)), AXES, swap
        )
        for at, width in zip(OFFSETS, WIDTHS)
    ]

    sent_kv, sent_q = vmem_call(
        sort_kernel,
        (shape(ROWS, 3 * DH), shape(ROWS, HQ * DH)),
        operands=(dest, qkv_in[0]),
        flops=10**9,
        nbytes=3 * MIB,
    )
    got_kv = lax.all_to_all(
        sent_kv.reshape(GROUPS, ROWS // GROUPS, 3 * DH), "dp", 0, 0, tiled=True
    ).reshape(ROWS, 3 * DH)
    got_q = lax.all_to_all(
        sent_q.reshape(GROUPS, ROWS // GROUPS, HQ * DH), "dp", 0, 0, tiled=True
    ).reshape(ROWS, HQ * DH)
    key_vals, inverse = vmem_call(
        place_kernel,
        (shape(ROWS, 2 * DH), shape(ROWS, ROWS)),
        operands=(got_kv,),
        flops=2 * 10**8,
        nbytes=MIB,
    )
    earlier = [
        lax.ppermute(key_vals, "ctx", [(at, at + back) for at in range(SLOTS - back)])
        for back in range(1, BACK + 1)
    ]

    flips = jnp.asarray(flip_table())
    flips = jnp.where(core == 0, flips, flips[::-1])
    to_x, to_y, to_z = x ^ flips[..., 0], y ^ flips[..., 1], z ^ flips[..., 2]
    table = ((to_y * 2 + to_z // 2) * 128 + ((to_z % 2) * 4 + to_x) * 8).astype(jnp.int32)

    (table, inverse, got_q, key_vals, earlier), own_cols, other_cols = lax.optimization_barrier(
        ((table, inverse, got_q, key_vals, earlier), own_cols, other_cols)
    )
    attention, left, swap_left = vmem_call(
        attend_kernel,
        (shape(ROWS, HQ * DH), shape(HQ * DH, ROWS), shape(HQ * DH, ROWS)),
        scratch=(
            pltpu.VMEM((ROWS, HQ * DH), jnp.bfloat16),
            pltpu.VMEM(((BACK + 1) * ROWS, DH), jnp.bfloat16),
            pltpu.VMEM(((BACK + 1) * ROWS, 2 * DH), jnp.bfloat16),
            pltpu.VMEM((HQ * TILE, DH), jnp.float32),
            pltpu.VMEM((HQ * TILE, 2 * DH), jnp.float32),
            pltpu.VMEM((HQ * DH, ROWS), jnp.float32),
        ),
        smem=3,
        operands=(slot.reshape(1), lengths, table, inverse, got_q, key_vals, *earlier),
        mib=24,
        flops=10**10,
        nbytes=6 * MIB,
    )
    left2 = lax.ppermute(swap_left, AXES, swap)

    def project(part, half):
        return vmem_call(
            functools.partial(project_kernel, part, half),
            shape(512, WIDTHS[part]),
            operands=(left, left2, own_cols[part], other_cols[part]),
            flops=2 * 512 * 1024 * WIDTHS[part],
            nbytes=5 * MIB,
        )

    sends = [project(part, 1) for part in range(3)]
    coming = [
        lax.ppermute(sends[part], AXES, flip_pairs([ORDERS[c][part][0] for c in range(2)]))
        for part in range(3)
    ]
    keeps = [project(part, 0) for part in range(3)]
    for level in range(1, 4):
        sums = [
            keep.astype(jnp.float32) + came.astype(jnp.float32)
            for keep, came in zip(keeps, coming)
        ]
        lead = [2 if (level, part) == (1, 1) else 1 for part in range(3)]
        sums = [
            total.reshape(ahead, 2, -1, total.shape[1]) for ahead, total in zip(lead, sums)
        ]
        keeps = [total[:, 0].reshape(-1, total.shape[-1]) for total in sums]
        sends = [total[:, 1].reshape(-1, total.shape[-1]).astype(jnp.bfloat16) for total in sums]
        if level < 3:
            coming = [
                lax.ppermute(
                    sends[part], AXES, flip_pairs([ORDERS[c][part][level] for c in range(2)])
                )
                for part in range(3)
            ]
    keep, send = jnp.concatenate(keeps, axis=1), jnp.concatenate(sends, axis=1)
    for level in range(3, 6):
        came = lax.ppermute(send, AXES, flip_pairs([ORDERS[c][0][level] for c in range(2)]))
        total = keep + came.astype(jnp.float32)
        rows = total.shape[0] // 2
        keep, send = total[:rows], total[rows:].astype(jnp.bfloat16)
    both = total.reshape(2, 8, HALF)
    mine = lax.dynamic_index_in_dim(both, core, 0, keepdims=False)
    theirs = lax.dynamic_index_in_dim(both, 1 - core, 0, keepdims=False).astype(jnp.bfloat16)
    came = lax.ppermute(theirs, AXES, swap).astype(jnp.float32)
    grad_proj = jnp.where(
        core == 0,
        jnp.concatenate([mine, came], axis=1),
        jnp.concatenate([came, mine], axis=1),
    )
    return attention[None], grad_proj


def solution(mesh):
    in_specs = (P("dp", "ctx", None), P("dp", "ctx"), P("dp", None), P("dp", "ctx", None))
    out_specs = (P("dp", "ctx", None), P(("dp", "ctx"), None))
    return jax.shard_map(body, mesh=mesh, in_specs=in_specs, out_specs=out_specs, check_vma=False)
```

```python
import functools

import jax
import jax.numpy as jnp
import numpy as np
from jax import lax
from jax.experimental import pallas as pl
from jax.experimental.pallas import tpu as pltpu
from jax.sharding import PartitionSpec as P

HQ = 8
DH = 128
ROWS = 512
GROUPS = 16
SLOTS = 8
BACK = 4
QUERIES = HQ * DH
HEAD = 3 * DH
SENT = QUERIES + HEAD
TILE = 256
AXES = ("dp", "ctx")
CHIPS = 64
MIB = 1024 * 1024
SCORE_FLOOR = -1e30
TOTAL_LIMIT = 2.0**90
EXP_SCALE = float(DH**-0.5 * np.log2(np.e))
WIDTHS = (1536, 1408, 1152)
OFFSETS = (0, 1536, 2944)
HALF = 4096

FLIPS = {
    "xa": (1, 0, 0),
    "xb": (3, 0, 0),
    "ya": (0, 1, 0),
    "yb": (0, 3, 0),
    "za": (0, 0, 1),
    "zb": (0, 0, 3),
}
SET_A = ("xa", "ya", "za")
SET_B = ("xb", "yb", "zb")


def rotate(names, by):
    return names[by:] + names[:by]


ORDERS = (
    tuple(rotate(SET_A, part) + SET_B for part in range(3)),
    tuple(rotate(SET_B, part) + SET_A for part in range(3)),
)


def place_of(index):
    dp, ctx = index // SLOTS, index % SLOTS
    y, z_hi, core = dp // 4, (dp // 2) % 2, dp % 2
    return ctx % 4, y, z_hi * 2 + ctx // 4, core


def index_of(x, y, z, core):
    return (y * 4 + (z // 2) * 2 + core) * SLOTS + (z % 2) * 4 + x


def flip_of(names):
    flips = [FLIPS[name] for name in names]
    return [functools.reduce(lambda a, b: a ^ b, axis) for axis in zip(*flips)]


def flip_pairs(names_of_core):
    pairs = []
    for index in range(2 * CHIPS):
        x, y, z, core = place_of(index)
        names = names_of_core[core]
        fx, fy, fz = flip_of((names,) if isinstance(names, str) else names)
        pairs.append((index, index_of(x ^ fx, y ^ fy, z ^ fz, core)))
    return pairs


def core_pairs():
    pairs = []
    for index in range(2 * CHIPS):
        x, y, z, core = place_of(index)
        pairs.append((index, index_of(x, y, z, 1 - core)))
    return pairs


def flip_table():
    table = np.zeros((2, CHIPS, 3), np.int32)
    for core in range(2):
        for block in range(CHIPS):
            for level, name in enumerate(ORDERS[core][0]):
                if (block >> (5 - level)) & 1:
                    table[core, block] ^= np.array(FLIPS[name], np.int32)
    return table


def dot(a, b, contract):
    return lax.dot_general(
        a, b, ((contract[:1], contract[1:]), ((), ())), preferred_element_type=jnp.float32
    )


def as_bf16(mask):
    return mask.astype(jnp.float32).astype(jnp.bfloat16)


def vmem_call(body, out_shape, scratch=(), smem=0, operands=(), mib=16, flops=0, nbytes=0):
    specs = [pl.BlockSpec(memory_space=pltpu.SMEM)] * smem
    specs += [pl.BlockSpec(memory_space=pltpu.VMEM)] * (len(operands) - smem)
    out_specs = jax.tree.map(lambda _: pl.BlockSpec(memory_space=pltpu.VMEM), out_shape)
    return pl.pallas_call(
        body,
        out_shape=out_shape,
        in_specs=specs,
        out_specs=out_specs,
        scratch_shapes=list(scratch),
        compiler_params=pltpu.CompilerParams(vmem_limit_bytes=mib * MIB),
        cost_estimate=pl.CostEstimate(flops=flops, bytes_accessed=nbytes, transcendentals=0),
    )(*operands)


def sort_kernel(dest_ref, rows_ref, sent_ref, held_ref, sem_ref):
    rows_copy = pltpu.make_async_copy(rows_ref.at[0], held_ref, sem_ref)
    rows_copy.start()
    dest = dest_ref[...]
    target = dest >> 9
    slot = dest & (ROWS - 1)
    member = as_bf16(lax.broadcasted_iota(jnp.int32, (GROUPS, ROWS), 0) == target)
    same = dot(member, member, (0, 0))
    row = lax.broadcasted_iota(jnp.int32, (ROWS, ROWS), 0)
    col = lax.broadcasted_iota(jnp.int32, (ROWS, ROWS), 1)
    rank = jnp.sum(jnp.where(row < col, same, 0.0), axis=0, keepdims=True)
    place = target * (ROWS // GROUPS) + rank.astype(jnp.int32)
    order = as_bf16(row == place)
    line = lax.broadcasted_iota(jnp.int32, (DH, ROWS), 0)
    coded = jnp.where(line == 0, slot >> 4, jnp.where(line == 1, slot & 15, 0))
    coded = coded.astype(jnp.float32).astype(jnp.bfloat16)
    sent_ref[:, 2 * DH : HEAD] = dot(order, coded, (1, 1)).astype(jnp.bfloat16)
    rows_copy.wait()
    sent_ref[:, : 2 * DH] = dot(order, held_ref[:, QUERIES:], (1, 0)).astype(jnp.bfloat16)
    sent_ref[:, HEAD:] = dot(order, held_ref[:, :QUERIES], (1, 0)).astype(jnp.bfloat16)


def place_kernel(got_ref, key_vals_ref, inverse_ref):
    lane = lax.broadcasted_iota(jnp.int32, (16, DH), 1)
    coef = jnp.where(lane == 0, 16.0, jnp.where(lane == 1, 1.0, 0.0)).astype(jnp.bfloat16)
    slots = dot(coef, got_ref[:, 2 * DH :], (1, 1))[:1].astype(jnp.int32)
    inverse = as_bf16(lax.broadcasted_iota(jnp.int32, (ROWS, ROWS), 0) == slots)
    inverse_ref[...] = inverse
    key_vals_ref[...] = dot(
        inverse, got_ref[:, : 2 * DH], (1, 0)
    ).astype(jnp.bfloat16)


def doc_starts(lengths_ref):
    start1 = lengths_ref[0, 0]
    start2 = start1 + lengths_ref[0, 1]
    start3 = start2 + lengths_ref[0, 2]

    def first_of(position):
        found = jnp.where(position >= start1, start1, 0)
        found = jnp.where(position >= start2, start2, found)
        return jnp.where(position >= start3, start3, found)

    return first_of


def visible_keys(first_of, p_first, k_first):
    q_pos = p_first + lax.broadcasted_iota(jnp.int32, (TILE, TILE), 0)
    k_pos = k_first + lax.broadcasted_iota(jnp.int32, (TILE, TILE), 1)
    return (k_pos >= first_of(q_pos)) & (k_pos <= q_pos)


def tile_weights(queries, keys, top, visible):
    scores = dot(queries, keys, (1, 1))
    if visible is not None:
        scores = jnp.where(visible, scores, SCORE_FLOOR)
    top = jnp.concatenate([top] * (scores.shape[1] // DH), axis=1)
    return jnp.exp2(scores * EXP_SCALE - top).astype(jnp.bfloat16)


def rows_of(h, tile=0):
    return slice((tile * HQ + h) * TILE, (tile * HQ + h + 1) * TILE)


def cols_of(h):
    return slice(h * DH, (h + 1) * DH)


def own_kernel(slot_ref, lengths_ref, inverse_ref, got_ref, kv_ref, q_ref, top_ref, acc_ref, v_ref):
    q_ref[...] = dot(inverse_ref[...], got_ref[:, HEAD:], (1, 0)).astype(jnp.bfloat16)
    v_ref[:, :DH] = kv_ref[:, DH:]
    v_ref[:, DH:] = jnp.ones((ROWS, DH), jnp.bfloat16)
    first_of = doc_starts(lengths_ref)
    ones = jnp.ones((DH, DH), jnp.bfloat16)
    for tile in range(ROWS // TILE):
        q_rows = slice(tile * TILE, (tile + 1) * TILE)
        p_first = slot_ref[0] * ROWS + tile * TILE
        own_keys = kv_ref[q_rows, :DH].astype(jnp.float32)
        for h in range(HQ):
            pair = q_ref[q_rows, cols_of(h)].astype(jnp.float32) * own_keys
            top_ref[rows_of(h, tile), :] = (
                dot(pair.astype(jnp.bfloat16), ones, (1, 0)) * EXP_SCALE
            )
        for at in range(tile, -1, -1):
            k_rows = slice(at * TILE, (at + 1) * TILE)
            visible = visible_keys(first_of, p_first, slot_ref[0] * ROWS + at * TILE)
            for h in range(HQ):
                weights = tile_weights(
                    q_ref[q_rows, cols_of(h)],
                    kv_ref[k_rows, :DH],
                    top_ref[rows_of(h, tile), :],
                    visible,
                )
                term = dot(weights, v_ref[k_rows, :], (1, 0))
                if at == tile:
                    acc_ref[rows_of(h, tile), :] = term
                else:
                    acc_ref[rows_of(h, tile), :] += term


def attend_kernel(
    slot_ref,
    lengths_ref,
    table_ref,
    q_ref,
    top_ref,
    total_ref,
    kv_ref,
    near0_ref,
    near1_ref,
    near2_ref,
    far0_ref,
    far1_ref,
    far2_ref,
    last_ref,
    *refs,
):
    grads, refs = refs[:6], refs[6:]
    (out_ref, own_ref, swap_ref), held, refs = refs[:3], refs[3:9], refs[9:]
    k_ref, v_ref, exact_ref, acc_ref, done_ref, sem_ref = refs
    copies = [
        pltpu.make_async_copy(grad_ref, held_ref, sem_ref.at[at])
        for at, (grad_ref, held_ref) in enumerate(zip(grads, held))
    ]
    for copy in copies:
        copy.start()
    slot = slot_ref[0]
    core = slot_ref[1]
    x = slot % 4
    k_ref[BACK * ROWS :, :] = kv_ref[:, :DH]
    v_ref[BACK * ROWS :, :DH] = kv_ref[:, DH:]
    v_ref[:, DH:] = jnp.ones(((BACK + 1) * ROWS, DH), jnp.bfloat16)
    came = (
        (near0_ref, (1, 0), (3, 0)),
        (near1_ref, (3, 0), (0, 1)),
        (near2_ref, (0, 1), (1, 0)),
        (far0_ref, (2, 0), (2, 0)),
        (far1_ref, (3, 1), (3, 1)),
        (far2_ref, (1, 1), (1, 1)),
        (last_ref, (2, 1), (2, 1)),
    )
    for came_ref, flip0, flip1 in came:
        flip_x = jnp.where(core == 0, flip0[0], flip1[0])
        flip_z = jnp.where(core == 0, flip0[1], flip1[1])
        back = slot - ((slot // 4) ^ flip_z) * 4 - (x ^ flip_x)

        @pl.when((back >= 1) & (back <= BACK))
        def _(came_ref=came_ref, back=back):
            at = pl.ds(pl.multiple_of((BACK - back) * ROWS, ROWS), ROWS)
            k_ref[at, :] = came_ref[:, :DH]
            v_ref[at, :DH] = came_ref[:, DH:]

    first_of = doc_starts(lengths_ref)
    for tile in range(ROWS // TILE):
        q_rows = slice(tile * TILE, (tile + 1) * TILE)
        p_first = slot * ROWS + tile * TILE
        low_first = first_of(p_first)
        high_first = first_of(p_first + TILE - 1)
        own_at = BACK * ROWS + tile * TILE
        count = (p_first - low_first + TILE - 1) // TILE
        clear = jnp.maximum(p_first - high_first, 0) // TILE
        acc_ref[...] = total_ref[tile * HQ * TILE : (tile + 1) * HQ * TILE, :]

        def add(j, masked, wide=1, tile=tile, q_rows=q_rows, p_first=p_first, own_at=own_at):
            at = pl.ds(pl.multiple_of(own_at - j * TILE, TILE), wide * TILE)
            visible = visible_keys(first_of, p_first, p_first - j * TILE) if masked else None
            for h in range(HQ):
                weights = tile_weights(
                    q_ref[q_rows, cols_of(h)], k_ref[at, :], top_ref[rows_of(h, tile), :], visible
                )
                acc_ref[rows_of(h), :] += dot(weights, v_ref[at, :], (1, 0))

        clear = jnp.maximum(clear, tile)

        pairs = (clear - tile) // 2

        @pl.loop(0, pairs)
        def _(i):
            add(2 + tile + 2 * i, False, 2)

        @pl.loop(1 + tile + 2 * pairs, 1 + clear)
        def _(j):
            add(j, False)

        @pl.loop(1 + clear, 1 + count)
        def _(j):
            add(j, True)

        @pl.when(jnp.max(acc_ref[:, DH:]) > TOTAL_LIMIT)
        def _(q_rows=q_rows, p_first=p_first, own_at=own_at, count=count):
            exact_ref[...] = jnp.full_like(exact_ref, SCORE_FLOOR)
            acc_ref[...] = jnp.zeros_like(acc_ref)

            @pl.loop(0, 1 + count)
            def _(j):
                at = pl.ds(pl.multiple_of(own_at - j * TILE, TILE), TILE)
                visible = visible_keys(first_of, p_first, p_first - j * TILE)

                @pl.loop(0, HQ)
                def _(h):
                    rows = pl.ds(pl.multiple_of(h * TILE, TILE), TILE)
                    cols = pl.ds(pl.multiple_of(h * DH, DH), DH)
                    scores = dot(q_ref[q_rows, cols], k_ref[at, :], (1, 1))
                    scores = jnp.where(visible, scores, SCORE_FLOOR)
                    old = exact_ref[rows, :]
                    best = jnp.max(scores, axis=1, keepdims=True) * EXP_SCALE
                    top = jnp.maximum(old, best)
                    rescale = jnp.exp2(old - top)
                    exact_ref[rows, :] = top
                    weights = tile_weights(q_ref[q_rows, cols], k_ref[at, :], top, visible)
                    rescale = jnp.concatenate([rescale, rescale], axis=1)
                    acc_ref[rows, :] = acc_ref[rows, :] * rescale + dot(
                        weights, v_ref[at, :], (1, 0)
                    )

        for h in range(HQ):
            done = acc_ref[rows_of(h), :DH] / acc_ref[rows_of(h), DH:]
            out_ref[q_rows, cols_of(h)] = done.astype(jnp.bfloat16)
            done_ref[cols_of(h), q_rows] = done.T

    for side, ordered_ref in enumerate((own_ref, swap_ref)):

        @pl.loop(0, CHIPS, unroll=4)
        def _(block, side=side, ordered_ref=ordered_ref):
            at = pl.multiple_of(table_ref[side, block], 8)
            both = jnp.concatenate(
                [done_ref[pl.ds(at, 8), :], done_ref[pl.ds(at + 64, 8), :]], axis=0
            )
            ordered_ref[pl.ds(pl.multiple_of(block * 16, 16), 16), :] = both.astype(jnp.bfloat16)
    for copy in copies:
        copy.wait()


def project_kernel(level, half, left_ref, left2_ref, own_ref, other_ref, out_ref):
    run = 512 >> level
    step = min(run, 256)
    for at in range(0, 512, step):
        rows = slice(at, at + step)
        source = (at // run) * 2 * run + half * run + at % run
        source = slice(source, source + step)
        term = dot(left_ref[source, :], own_ref[...], (1, 0))
        term += dot(left2_ref[source, :], other_ref[...], (1, 0))
        out_ref[rows, :] = term.astype(out_ref.dtype)


def shape(rows, cols, dtype=jnp.bfloat16):
    return jax.ShapeDtypeStruct((rows, cols), dtype)


def body(qkv_in, dest, lengths, grad_out):
    dp_at = lax.axis_index("dp")
    slot = lax.axis_index("ctx")
    core = dp_at % 2
    x, y, z = slot % 4, dp_at // 4, ((dp_at // 2) % 2) * 2 + slot // 4
    swap = core_pairs()

    tokens = grad_out[0]
    own_cols = [
        lax.dynamic_slice(tokens, (0, core * HALF + at), (ROWS, width))
        for at, width in zip(OFFSETS, WIDTHS)
    ]
    other_cols = [
        lax.ppermute(
            lax.dynamic_slice(tokens, (0, (1 - core) * HALF + at), (ROWS, width)), AXES, swap
        )
        for at, width in zip(OFFSETS, WIDTHS)
    ]

    sent = pl.pallas_call(
        sort_kernel,
        out_shape=shape(ROWS, SENT),
        in_specs=[
            pl.BlockSpec(memory_space=pltpu.VMEM),
            pl.BlockSpec(memory_space=pltpu.HBM),
        ],
        out_specs=pl.BlockSpec(memory_space=pltpu.VMEM),
        scratch_shapes=[
            pltpu.VMEM((ROWS, QUERIES + 2 * DH), jnp.bfloat16),
            pltpu.SemaphoreType.DMA,
        ],
        compiler_params=pltpu.CompilerParams(vmem_limit_bytes=60 * MIB),
        cost_estimate=pl.CostEstimate(flops=10**9, bytes_accessed=3 * MIB, transcendentals=0),
    )(dest, qkv_in)
    got = lax.all_to_all(
        sent.reshape(GROUPS, ROWS // GROUPS, SENT), "dp", 0, 0, tiled=True
    ).reshape(ROWS, SENT)
    key_vals, inverse = pl.pallas_call(
        place_kernel,
        grid=(1,),
        out_shape=(shape(ROWS, 2 * DH), shape(ROWS, ROWS)),
        in_specs=[pl.BlockSpec((ROWS, HEAD), lambda _: (0, 0))],
        out_specs=(
            pl.BlockSpec((ROWS, 2 * DH), lambda _: (0, 0)),
            pl.BlockSpec((ROWS, ROWS), lambda _: (0, 0)),
        ),
        compiler_params=pltpu.CompilerParams(vmem_limit_bytes=8 * MIB),
        cost_estimate=pl.CostEstimate(flops=2 * 10**8, bytes_accessed=MIB, transcendentals=0),
    )(got)
    near0 = lax.ppermute(key_vals, AXES, flip_pairs(("xa", "xb")))
    near1 = lax.ppermute(key_vals, AXES, flip_pairs(("xb", "za")))
    near2 = lax.ppermute(key_vals, AXES, flip_pairs(("za", "xa")))
    far0 = lax.ppermute(near0, AXES, flip_pairs(("xb", "xa")))
    far1 = lax.ppermute(near1, AXES, flip_pairs(("za", "xb")))
    far2 = lax.ppermute(near2, AXES, flip_pairs(("xa", "za")))
    last = lax.ppermute(far0, AXES, flip_pairs(("za", "za")))

    place = jnp.stack([slot, core]).astype(jnp.int32)
    queries, tops, totals = vmem_call(
        own_kernel,
        (
            shape(ROWS, QUERIES),
            shape(2 * HQ * TILE, DH, jnp.float32),
            shape(2 * HQ * TILE, 2 * DH, jnp.float32),
        ),
        scratch=(pltpu.VMEM((ROWS, 2 * DH), jnp.bfloat16),),
        smem=2,
        operands=(place, lengths, inverse, got, key_vals),
        mib=20,
        flops=2 * 10**9,
        nbytes=4 * MIB,
    )

    flips = jnp.asarray(flip_table())
    flips = jnp.where(core == 0, flips, flips[::-1])
    to_x, to_y, to_z = x ^ flips[..., 0], y ^ flips[..., 1], z ^ flips[..., 2]
    table = ((to_y * 2 + to_z // 2) * 128 + ((to_z % 2) * 4 + to_x) * 8).astype(jnp.int32)

    (table, queries, last), own_cols, other_cols = lax.optimization_barrier(
        ((table, queries, last), own_cols, other_cols)
    )
    vmem = pl.BlockSpec(memory_space=pltpu.VMEM)
    smem = pl.BlockSpec(memory_space=pltpu.SMEM)
    columns = (*own_cols, *other_cols)
    attention, left, swap_left, *columns = pl.pallas_call(
        attend_kernel,
        out_shape=(
            shape(ROWS, QUERIES),
            shape(QUERIES, ROWS),
            shape(QUERIES, ROWS),
            *(shape(*a.shape) for a in columns),
        ),
        in_specs=[smem] * 3 + [vmem] * 11 + [pl.BlockSpec(memory_space=pltpu.HBM)] * 6,
        out_specs=(vmem,) * 9,
        scratch_shapes=[
            pltpu.VMEM(((BACK + 1) * ROWS, DH), jnp.bfloat16),
            pltpu.VMEM(((BACK + 1) * ROWS, 2 * DH), jnp.bfloat16),
            pltpu.VMEM((HQ * TILE, DH), jnp.float32),
            pltpu.VMEM((HQ * TILE, 2 * DH), jnp.float32),
            pltpu.VMEM((QUERIES, ROWS), jnp.float32),
            pltpu.SemaphoreType.DMA((6,)),
        ],
        compiler_params=pltpu.CompilerParams(vmem_limit_bytes=28 * MIB),
        cost_estimate=pl.CostEstimate(
            flops=10**10, bytes_accessed=16 * MIB, transcendentals=0
        ),
    )(
        place,
        lengths,
        table,
        queries,
        tops,
        totals,
        key_vals,
        near0,
        near1,
        near2,
        far0,
        far1,
        far2,
        last,
        *columns,
    )
    own_cols, other_cols = columns[:3], columns[3:]
    left2 = lax.ppermute(swap_left, AXES, swap)

    def project(part, half):
        return vmem_call(
            functools.partial(project_kernel, part, half),
            shape(512, WIDTHS[part]),
            operands=(left, left2, own_cols[part], other_cols[part]),
            flops=2 * 512 * 1024 * WIDTHS[part],
            nbytes=5 * MIB,
        )

    sends = []
    for part in range(3):
        sends.append(project(part, 1))
        left, _ = lax.optimization_barrier((left, sends[-1]))
    keeps = [project(part, 0) for part in range(3)]
    for level in range(3):
        coming = [
            lax.ppermute(
                sends[part], AXES, flip_pairs([ORDERS[c][part][level] for c in range(2)])
            )
            for part in range(3)
        ]
        coming, keeps = lax.optimization_barrier((coming, keeps))
        halves = []
        for part in range(3):
            lead = 2 if (level, part) == (0, 1) else 1
            width = WIDTHS[part]
            halves.append(
                [
                    [a.reshape(lead, 2, -1, width)[:, bit].reshape(-1, width).astype(jnp.float32)
                     for a in (keeps[part], coming[part])]
                    for bit in range(2)
                ]
            )
        sends = [(pair[1][0] + pair[1][1]).astype(jnp.bfloat16) for pair in halves]
        keeps = [pair[0][0] + pair[0][1] for pair in halves]
    keep, send = jnp.concatenate(keeps, axis=1), jnp.concatenate(sends, axis=1)
    for level in range(3, 4):
        came = lax.ppermute(send, AXES, flip_pairs([ORDERS[c][0][level] for c in range(2)]))
        total = keep + came.astype(jnp.float32)
        rows = total.shape[0] // 2
        keep, send = total[:rows], total[rows:].astype(jnp.bfloat16)
    blocks = total.reshape(-1, 16, HALF)
    coming = []
    for block in range(blocks.shape[0] - 1, 0, -1):
        names = [
            [ORDERS[c][0][5 - bit] for bit in range(2) if (block >> bit) & 1]
            for c in range(2)
        ]
        coming.append(lax.ppermute(blocks[block].astype(jnp.bfloat16), AXES, flip_pairs(names)))
    coming = lax.optimization_barrier(coming)
    total = blocks[0]
    for came in coming:
        total = total + came.astype(jnp.float32)
    both = total.reshape(2, 8, HALF)
    mine = lax.dynamic_index_in_dim(both, core, 0, keepdims=False)
    theirs = lax.dynamic_index_in_dim(both, 1 - core, 0, keepdims=False).astype(jnp.bfloat16)
    came = lax.ppermute(theirs, AXES, swap).astype(jnp.float32)
    grad_proj = jnp.where(
        core == 0,
        jnp.concatenate([mine, came], axis=1),
        jnp.concatenate([came, mine], axis=1),
    )
    return attention[None], grad_proj


def solution(mesh):
    in_specs = (P("dp", "ctx", None), P("dp", "ctx"), P("dp", None), P("dp", "ctx", None))
    out_specs = (P("dp", "ctx", None), P(("dp", "ctx"), None))
    return jax.shard_map(body, mesh=mesh, in_specs=in_specs, out_specs=out_specs, check_vma=False)
```

```python
import functools

import jax
import jax.numpy as jnp
import numpy as np
from jax import lax
from jax.experimental import pallas as pl
from jax.experimental.pallas import tpu as pltpu
from jax.sharding import PartitionSpec as P

HQ = 8
DH = 128
ROWS = 512
GROUPS = 16
SLOTS = 8
BACK = 4
QUERIES = HQ * DH
HEAD = 3 * DH
SENT = QUERIES + HEAD
TILE = 256
AXES = ("dp", "ctx")
CHIPS = 64
MIB = 1024 * 1024
SCORE_FLOOR = -1e30
TOTAL_LIMIT = 2.0**90
EXP_SCALE = float(DH**-0.5 * np.log2(np.e))
WIDTHS = (1536, 1408, 1152)
OFFSETS = (0, 1536, 2944)
HALF = 4096

FLIPS = {
    "xa": (1, 0, 0),
    "xb": (3, 0, 0),
    "ya": (0, 1, 0),
    "yb": (0, 3, 0),
    "za": (0, 0, 1),
    "zb": (0, 0, 3),
}
SET_A = ("xa", "ya", "za")
SET_B = ("xb", "yb", "zb")


def rotate(names, by):
    return names[by:] + names[:by]


ORDERS = (
    tuple(rotate(SET_A, part) + SET_B for part in range(3)),
    tuple(rotate(SET_B, part) + SET_A for part in range(3)),
)


def place_of(index):
    dp, ctx = index // SLOTS, index % SLOTS
    y, z_hi, core = dp // 4, (dp // 2) % 2, dp % 2
    return ctx % 4, y, z_hi * 2 + ctx // 4, core


def index_of(x, y, z, core):
    return (y * 4 + (z // 2) * 2 + core) * SLOTS + (z % 2) * 4 + x


def flip_of(names):
    flips = [FLIPS[name] for name in names]
    return [functools.reduce(lambda a, b: a ^ b, axis) for axis in zip(*flips)]


def flip_pairs(names_of_core):
    pairs = []
    for index in range(2 * CHIPS):
        x, y, z, core = place_of(index)
        names = names_of_core[core]
        fx, fy, fz = flip_of((names,) if isinstance(names, str) else names)
        pairs.append((index, index_of(x ^ fx, y ^ fy, z ^ fz, core)))
    return pairs


def core_pairs():
    pairs = []
    for index in range(2 * CHIPS):
        x, y, z, core = place_of(index)
        pairs.append((index, index_of(x, y, z, 1 - core)))
    return pairs


def flip_table():
    table = np.zeros((2, CHIPS, 3), np.int32)
    for core in range(2):
        for block in range(CHIPS):
            for level, name in enumerate(ORDERS[core][0]):
                if (block >> (5 - level)) & 1:
                    table[core, block] ^= np.array(FLIPS[name], np.int32)
    return table


def dot(a, b, contract):
    return lax.dot_general(
        a, b, ((contract[:1], contract[1:]), ((), ())), preferred_element_type=jnp.float32
    )


def as_bf16(mask):
    return mask.astype(jnp.float32).astype(jnp.bfloat16)


def vmem_call(body, out_shape, scratch=(), smem=0, operands=(), mib=16, flops=0, nbytes=0):
    specs = [pl.BlockSpec(memory_space=pltpu.SMEM)] * smem
    specs += [pl.BlockSpec(memory_space=pltpu.VMEM)] * (len(operands) - smem)
    out_specs = jax.tree.map(lambda _: pl.BlockSpec(memory_space=pltpu.VMEM), out_shape)
    return pl.pallas_call(
        body,
        out_shape=out_shape,
        in_specs=specs,
        out_specs=out_specs,
        scratch_shapes=list(scratch),
        compiler_params=pltpu.CompilerParams(vmem_limit_bytes=mib * MIB),
        cost_estimate=pl.CostEstimate(flops=flops, bytes_accessed=nbytes, transcendentals=0),
    )(*operands)


def sort_kernel(dest_ref, rows_ref, sent_ref, held_ref, sem_ref):
    rows_copy = pltpu.make_async_copy(rows_ref.at[0], held_ref, sem_ref)
    rows_copy.start()
    dest = dest_ref[...]
    target = dest >> 9
    slot = dest & (ROWS - 1)
    member = as_bf16(lax.broadcasted_iota(jnp.int32, (GROUPS, ROWS), 0) == target)
    same = dot(member, member, (0, 0))
    row = lax.broadcasted_iota(jnp.int32, (ROWS, ROWS), 0)
    col = lax.broadcasted_iota(jnp.int32, (ROWS, ROWS), 1)
    rank = jnp.sum(jnp.where(row < col, same, 0.0), axis=0, keepdims=True)
    place = target * (ROWS // GROUPS) + rank.astype(jnp.int32)
    order = as_bf16(row == place)
    line = lax.broadcasted_iota(jnp.int32, (DH, ROWS), 0)
    coded = jnp.where(line == 0, slot >> 4, jnp.where(line == 1, slot & 15, 0))
    coded = coded.astype(jnp.float32).astype(jnp.bfloat16)
    sent_ref[:, 2 * DH : HEAD] = dot(order, coded, (1, 1)).astype(jnp.bfloat16)
    rows_copy.wait()
    sent_ref[:, : 2 * DH] = dot(order, held_ref[:, QUERIES:], (1, 0)).astype(jnp.bfloat16)
    sent_ref[:, HEAD:] = dot(order, held_ref[:, :QUERIES], (1, 0)).astype(jnp.bfloat16)


def place_kernel(got_ref, key_vals_ref, inverse_ref):
    lane = lax.broadcasted_iota(jnp.int32, (16, DH), 1)
    coef = jnp.where(lane == 0, 16.0, jnp.where(lane == 1, 1.0, 0.0)).astype(jnp.bfloat16)
    slots = dot(coef, got_ref[:, 2 * DH :], (1, 1))[:1].astype(jnp.int32)
    inverse = as_bf16(lax.broadcasted_iota(jnp.int32, (ROWS, ROWS), 0) == slots)
    inverse_ref[...] = inverse
    key_vals_ref[...] = dot(
        inverse, got_ref[:, : 2 * DH], (1, 0)
    ).astype(jnp.bfloat16)


def doc_starts(lengths_ref):
    start1 = lengths_ref[0, 0]
    start2 = start1 + lengths_ref[0, 1]
    start3 = start2 + lengths_ref[0, 2]

    def first_of(position):
        found = jnp.where(position >= start1, start1, 0)
        found = jnp.where(position >= start2, start2, found)
        return jnp.where(position >= start3, start3, found)

    return first_of


def visible_keys(first_of, p_first, k_first):
    q_pos = p_first + lax.broadcasted_iota(jnp.int32, (TILE, TILE), 0)
    k_pos = k_first + lax.broadcasted_iota(jnp.int32, (TILE, TILE), 1)
    return (k_pos >= first_of(q_pos)) & (k_pos <= q_pos)


def tile_weights(queries, keys, top, visible):
    scores = dot(queries, keys, (1, 1))
    if visible is not None:
        scores = jnp.where(visible, scores, SCORE_FLOOR)
    top = jnp.concatenate([top] * (scores.shape[1] // DH), axis=1)
    return jnp.exp2(scores * EXP_SCALE - top).astype(jnp.bfloat16)


def rows_of(h, tile=0):
    return slice((tile * HQ + h) * TILE, (tile * HQ + h + 1) * TILE)


def cols_of(h):
    return slice(h * DH, (h + 1) * DH)


def own_kernel(slot_ref, lengths_ref, inverse_ref, got_ref, kv_ref, q_ref, top_ref, acc_ref, v_ref):
    q_ref[...] = dot(inverse_ref[...], got_ref[:, HEAD:], (1, 0)).astype(jnp.bfloat16)
    v_ref[:, :DH] = kv_ref[:, DH:]
    v_ref[:, DH:] = jnp.ones((ROWS, DH), jnp.bfloat16)
    first_of = doc_starts(lengths_ref)
    ones = jnp.ones((DH, DH), jnp.bfloat16)
    for tile in range(ROWS // TILE):
        q_rows = slice(tile * TILE, (tile + 1) * TILE)
        p_first = slot_ref[0] * ROWS + tile * TILE
        own_keys = kv_ref[q_rows, :DH].astype(jnp.float32)
        for h in range(HQ):
            pair = q_ref[q_rows, cols_of(h)].astype(jnp.float32) * own_keys
            top_ref[rows_of(h, tile), :] = (
                dot(pair.astype(jnp.bfloat16), ones, (1, 0)) * EXP_SCALE
            )
        for at in range(tile, -1, -1):
            k_rows = slice(at * TILE, (at + 1) * TILE)
            visible = visible_keys(first_of, p_first, slot_ref[0] * ROWS + at * TILE)
            for h in range(HQ):
                weights = tile_weights(
                    q_ref[q_rows, cols_of(h)],
                    kv_ref[k_rows, :DH],
                    top_ref[rows_of(h, tile), :],
                    visible,
                )
                term = dot(weights, v_ref[k_rows, :], (1, 0))
                if at == tile:
                    acc_ref[rows_of(h, tile), :] = term
                else:
                    acc_ref[rows_of(h, tile), :] += term


def attend_kernel(
    slot_ref,
    lengths_ref,
    table_ref,
    q_ref,
    top_ref,
    total_ref,
    kv_ref,
    near0_ref,
    near1_ref,
    near2_ref,
    far0_ref,
    far1_ref,
    far2_ref,
    last_ref,
    *refs,
):
    grads, refs = refs[:6], refs[6:]
    (out_ref, own_ref, swap_ref), held, refs = refs[:3], refs[3:9], refs[9:]
    k_ref, v_ref, exact_ref, acc_ref, done_ref, sem_ref = refs
    copies = [
        pltpu.make_async_copy(grad_ref, held_ref, sem_ref.at[at])
        for at, (grad_ref, held_ref) in enumerate(zip(grads, held))
    ]
    for copy in copies:
        copy.start()
    slot = slot_ref[0]
    core = slot_ref[1]
    x = slot % 4
    k_ref[BACK * ROWS :, :] = kv_ref[:, :DH]
    v_ref[BACK * ROWS :, :DH] = kv_ref[:, DH:]
    v_ref[:, DH:] = jnp.ones(((BACK + 1) * ROWS, DH), jnp.bfloat16)
    came = (
        (near0_ref, (1, 0), (3, 0)),
        (near1_ref, (3, 0), (0, 1)),
        (near2_ref, (0, 1), (1, 0)),
        (far0_ref, (2, 0), (2, 0)),
        (far1_ref, (3, 1), (3, 1)),
        (far2_ref, (1, 1), (1, 1)),
        (last_ref, (2, 1), (2, 1)),
    )
    for came_ref, flip0, flip1 in came:
        flip_x = jnp.where(core == 0, flip0[0], flip1[0])
        flip_z = jnp.where(core == 0, flip0[1], flip1[1])
        back = slot - ((slot // 4) ^ flip_z) * 4 - (x ^ flip_x)

        @pl.when((back >= 1) & (back <= BACK))
        def _(came_ref=came_ref, back=back):
            at = pl.ds(pl.multiple_of((BACK - back) * ROWS, ROWS), ROWS)
            k_ref[at, :] = came_ref[:, :DH]
            v_ref[at, :DH] = came_ref[:, DH:]

    first_of = doc_starts(lengths_ref)
    for tile in range(ROWS // TILE):
        q_rows = slice(tile * TILE, (tile + 1) * TILE)
        p_first = slot * ROWS + tile * TILE
        low_first = first_of(p_first)
        high_first = first_of(p_first + TILE - 1)
        own_at = BACK * ROWS + tile * TILE
        count = (p_first - low_first + TILE - 1) // TILE
        clear = jnp.maximum(p_first - high_first, 0) // TILE
        acc_ref[...] = total_ref[tile * HQ * TILE : (tile + 1) * HQ * TILE, :]

        def add(j, masked, wide=1, tile=tile, q_rows=q_rows, p_first=p_first, own_at=own_at):
            at = pl.ds(pl.multiple_of(own_at - j * TILE, TILE), wide * TILE)
            visible = visible_keys(first_of, p_first, p_first - j * TILE) if masked else None
            for h in range(HQ):
                weights = tile_weights(
                    q_ref[q_rows, cols_of(h)], k_ref[at, :], top_ref[rows_of(h, tile), :], visible
                )
                acc_ref[rows_of(h), :] += dot(weights, v_ref[at, :], (1, 0))

        clear = jnp.maximum(clear, tile)

        pairs = (clear - tile) // 2

        @pl.loop(0, pairs)
        def _(i):
            add(2 + tile + 2 * i, False, 2)

        @pl.loop(1 + tile + 2 * pairs, 1 + clear)
        def _(j):
            add(j, False)

        @pl.loop(1 + clear, 1 + count)
        def _(j):
            add(j, True)

        @pl.when(jnp.max(acc_ref[:, DH:]) > TOTAL_LIMIT)
        def _(q_rows=q_rows, p_first=p_first, own_at=own_at, count=count):
            exact_ref[...] = jnp.full_like(exact_ref, SCORE_FLOOR)
            acc_ref[...] = jnp.zeros_like(acc_ref)

            @pl.loop(0, 1 + count)
            def _(j):
                at = pl.ds(pl.multiple_of(own_at - j * TILE, TILE), TILE)
                visible = visible_keys(first_of, p_first, p_first - j * TILE)

                @pl.loop(0, HQ)
                def _(h):
                    rows = pl.ds(pl.multiple_of(h * TILE, TILE), TILE)
                    cols = pl.ds(pl.multiple_of(h * DH, DH), DH)
                    scores = dot(q_ref[q_rows, cols], k_ref[at, :], (1, 1))
                    scores = jnp.where(visible, scores, SCORE_FLOOR)
                    old = exact_ref[rows, :]
                    best = jnp.max(scores, axis=1, keepdims=True) * EXP_SCALE
                    top = jnp.maximum(old, best)
                    rescale = jnp.exp2(old - top)
                    exact_ref[rows, :] = top
                    weights = tile_weights(q_ref[q_rows, cols], k_ref[at, :], top, visible)
                    rescale = jnp.concatenate([rescale, rescale], axis=1)
                    acc_ref[rows, :] = acc_ref[rows, :] * rescale + dot(
                        weights, v_ref[at, :], (1, 0)
                    )

        for h in range(HQ):
            done = acc_ref[rows_of(h), :DH] / acc_ref[rows_of(h), DH:]
            out_ref[q_rows, cols_of(h)] = done.astype(jnp.bfloat16)
            done_ref[cols_of(h), q_rows] = done.T

    for side, ordered_ref in enumerate((own_ref, swap_ref)):

        @pl.loop(0, CHIPS, unroll=4)
        def _(block, side=side, ordered_ref=ordered_ref):
            at = pl.multiple_of(table_ref[side, block], 8)
            both = jnp.concatenate(
                [done_ref[pl.ds(at, 8), :], done_ref[pl.ds(at + 64, 8), :]], axis=0
            )
            ordered_ref[pl.ds(pl.multiple_of(block * 16, 16), 16), :] = both.astype(jnp.bfloat16)
    for copy in copies:
        copy.wait()


def project_kernel(level, half, left_ref, cols_ref, *refs):
    start_ref, out_ref = refs if len(refs) == 2 else (None, refs[0])
    run = 512 >> level
    step = min(run, 256)
    for at in range(0, 512, step):
        rows = slice(at, at + step)
        source = (at // run) * 2 * run + half * run + at % run
        term = dot(left_ref[source : source + step, :], cols_ref[...], (1, 0))
        if start_ref is not None:
            term += start_ref[rows, :]
        out_ref[rows, :] = term.astype(out_ref.dtype)


def shape(rows, cols, dtype=jnp.bfloat16):
    return jax.ShapeDtypeStruct((rows, cols), dtype)


def body(qkv_in, dest, lengths, grad_out):
    dp_at = lax.axis_index("dp")
    slot = lax.axis_index("ctx")
    core = dp_at % 2
    x, y, z = slot % 4, dp_at // 4, ((dp_at // 2) % 2) * 2 + slot // 4
    swap = core_pairs()

    tokens = grad_out[0]
    own_cols = [
        lax.dynamic_slice(tokens, (0, core * HALF + at), (ROWS, width))
        for at, width in zip(OFFSETS, WIDTHS)
    ]
    other_cols = [
        lax.ppermute(
            lax.dynamic_slice(tokens, (0, (1 - core) * HALF + at), (ROWS, width)), AXES, swap
        )
        for at, width in zip(OFFSETS, WIDTHS)
    ]

    sent = pl.pallas_call(
        sort_kernel,
        out_shape=shape(ROWS, SENT),
        in_specs=[
            pl.BlockSpec(memory_space=pltpu.VMEM),
            pl.BlockSpec(memory_space=pltpu.HBM),
        ],
        out_specs=pl.BlockSpec(memory_space=pltpu.VMEM),
        scratch_shapes=[
            pltpu.VMEM((ROWS, QUERIES + 2 * DH), jnp.bfloat16),
            pltpu.SemaphoreType.DMA,
        ],
        compiler_params=pltpu.CompilerParams(vmem_limit_bytes=60 * MIB),
        cost_estimate=pl.CostEstimate(flops=10**9, bytes_accessed=3 * MIB, transcendentals=0),
    )(dest, qkv_in)
    got = lax.all_to_all(
        sent.reshape(GROUPS, ROWS // GROUPS, SENT), "dp", 0, 0, tiled=True
    ).reshape(ROWS, SENT)
    key_vals, inverse = pl.pallas_call(
        place_kernel,
        grid=(1,),
        out_shape=(shape(ROWS, 2 * DH), shape(ROWS, ROWS)),
        in_specs=[pl.BlockSpec((ROWS, HEAD), lambda _: (0, 0))],
        out_specs=(
            pl.BlockSpec((ROWS, 2 * DH), lambda _: (0, 0)),
            pl.BlockSpec((ROWS, ROWS), lambda _: (0, 0)),
        ),
        compiler_params=pltpu.CompilerParams(vmem_limit_bytes=8 * MIB),
        cost_estimate=pl.CostEstimate(flops=2 * 10**8, bytes_accessed=MIB, transcendentals=0),
    )(got)
    near0 = lax.ppermute(key_vals, AXES, flip_pairs(("xa", "xb")))
    near1 = lax.ppermute(key_vals, AXES, flip_pairs(("xb", "za")))
    near2 = lax.ppermute(key_vals, AXES, flip_pairs(("za", "xa")))
    far0 = lax.ppermute(near0, AXES, flip_pairs(("xb", "xa")))
    far1 = lax.ppermute(near1, AXES, flip_pairs(("za", "xb")))
    far2 = lax.ppermute(near2, AXES, flip_pairs(("xa", "za")))
    last = lax.ppermute(far0, AXES, flip_pairs(("za", "za")))

    place = jnp.stack([slot, core]).astype(jnp.int32)
    queries, tops, totals = vmem_call(
        own_kernel,
        (
            shape(ROWS, QUERIES),
            shape(2 * HQ * TILE, DH, jnp.float32),
            shape(2 * HQ * TILE, 2 * DH, jnp.float32),
        ),
        scratch=(pltpu.VMEM((ROWS, 2 * DH), jnp.bfloat16),),
        smem=2,
        operands=(place, lengths, inverse, got, key_vals),
        mib=20,
        flops=2 * 10**9,
        nbytes=4 * MIB,
    )

    flips = jnp.asarray(flip_table())
    flips = jnp.where(core == 0, flips, flips[::-1])
    to_x, to_y, to_z = x ^ flips[..., 0], y ^ flips[..., 1], z ^ flips[..., 2]
    table = ((to_y * 2 + to_z // 2) * 128 + ((to_z % 2) * 4 + to_x) * 8).astype(jnp.int32)

    (table, queries, last), own_cols, other_cols = lax.optimization_barrier(
        ((table, queries, last), own_cols, other_cols)
    )
    vmem = pl.BlockSpec(memory_space=pltpu.VMEM)
    smem = pl.BlockSpec(memory_space=pltpu.SMEM)
    columns = (*own_cols, *other_cols)
    attention, left, swap_left, *columns = pl.pallas_call(
        attend_kernel,
        out_shape=(
            shape(ROWS, QUERIES),
            shape(QUERIES, ROWS),
            shape(QUERIES, ROWS),
            *(shape(*a.shape) for a in columns),
        ),
        in_specs=[smem] * 3 + [vmem] * 11 + [pl.BlockSpec(memory_space=pltpu.HBM)] * 6,
        out_specs=(vmem,) * 9,
        scratch_shapes=[
            pltpu.VMEM(((BACK + 1) * ROWS, DH), jnp.bfloat16),
            pltpu.VMEM(((BACK + 1) * ROWS, 2 * DH), jnp.bfloat16),
            pltpu.VMEM((HQ * TILE, DH), jnp.float32),
            pltpu.VMEM((HQ * TILE, 2 * DH), jnp.float32),
            pltpu.VMEM((QUERIES, ROWS), jnp.float32),
            pltpu.SemaphoreType.DMA((6,)),
        ],
        compiler_params=pltpu.CompilerParams(vmem_limit_bytes=20 * MIB),
        cost_estimate=pl.CostEstimate(
            flops=10**10, bytes_accessed=16 * MIB, transcendentals=0
        ),
    )(
        place,
        lengths,
        table,
        queries,
        tops,
        totals,
        key_vals,
        near0,
        near1,
        near2,
        far0,
        far1,
        far2,
        last,
        *columns,
    )
    own_cols, other_cols = columns[:3], columns[3:]
    left2 = lax.ppermute(swap_left, AXES, swap)

    def project(part, half, side, start, dtype):
        return vmem_call(
            functools.partial(project_kernel, part, half),
            shape(512, WIDTHS[part], dtype),
            operands=(side, *start),
            flops=2 * 512 * 512 * WIDTHS[part],
            nbytes=5 * MIB,
        )

    own_terms = [project(part, 1, left, (own_cols[part],), jnp.float32) for part in range(3)]
    sends = []
    for part in range(3):
        sends.append(project(part, 1, left2, (other_cols[part], own_terms[part]), jnp.bfloat16))
        left2, _ = lax.optimization_barrier((left2, sends[-1]))
    keeps = []
    for part in range(3):
        term = project(part, 0, left2, (other_cols[part],), jnp.float32)
        keeps.append(project(part, 0, left, (own_cols[part], term), jnp.bfloat16))
    coming = [
        lax.ppermute(sends[part], AXES, flip_pairs([ORDERS[c][part][0] for c in range(2)]))
        for part in range(3)
    ]
    keeps, coming[0] = lax.optimization_barrier((keeps, coming[0]))
    for level in range(3):
        for part in range(3):
            lead = 2 if (level, part) == (0, 1) else 1
            width = WIDTHS[part]
            came = coming[part]
            if True and part > 0:
                came, _ = lax.optimization_barrier((came, sends[part - 1]))
            halves = [
                [
                    a.reshape(lead, 2, -1, width)[:, bit].reshape(-1, width).astype(jnp.float32)
                    for a in (keeps[part], came)
                ]
                for bit in range(2)
            ]
            sends[part] = (halves[1][0] + halves[1][1]).astype(jnp.bfloat16)
            keeps[part] = halves[0][0] + halves[0][1]
            if level < 2:
                coming[part] = lax.ppermute(
                    sends[part],
                    AXES,
                    flip_pairs([ORDERS[c][part][level + 1] for c in range(2)]),
                )
    keep, send = jnp.concatenate(keeps, axis=1), jnp.concatenate(sends, axis=1)
    blocks = (
        (send[32:], (3, 4)),
        (send[:32], (3,)),
        (keep[32:].astype(jnp.bfloat16), (4,)),
    )
    coming = [
        lax.ppermute(
            block, AXES, flip_pairs([[ORDERS[c][0][level] for level in levels] for c in range(2)])
        )
        for block, levels in blocks
    ]
    coming = lax.optimization_barrier(coming)
    total = keep[:32]
    for came in coming:
        total = total + came.astype(jnp.float32)
    came = lax.ppermute(
        total[16:].astype(jnp.bfloat16), AXES, flip_pairs([ORDERS[c][0][5] for c in range(2)])
    )
    total = total[:16] + came.astype(jnp.float32)
    both = total.reshape(2, 8, HALF)
    mine = lax.dynamic_index_in_dim(both, core, 0, keepdims=False)
    theirs = lax.dynamic_index_in_dim(both, 1 - core, 0, keepdims=False).astype(jnp.bfloat16)
    came = lax.ppermute(theirs, AXES, swap).astype(jnp.float32)
    grad_proj = jnp.where(
        core == 0,
        jnp.concatenate([mine, came], axis=1),
        jnp.concatenate([came, mine], axis=1),
    )
    return attention[None], grad_proj


def solution(mesh):
    in_specs = (P("dp", "ctx", None), P("dp", "ctx"), P("dp", None), P("dp", "ctx", None))
    out_specs = (P("dp", "ctx", None), P(("dp", "ctx"), None))
    return jax.shard_map(body, mesh=mesh, in_specs=in_specs, out_specs=out_specs, check_vma=False)
```

```python
import functools

import jax
import jax.numpy as jnp
import numpy as np
from jax import lax
from jax.experimental import pallas as pl
from jax.experimental.pallas import tpu as pltpu
from jax.sharding import PartitionSpec as P

HQ = 8
DH = 128
ROWS = 512
GROUPS = 16
SLOTS = 8
BACK = 4
QUERIES = HQ * DH
HEAD = 3 * DH
SENT = QUERIES + HEAD
TILE = 256
AXES = ("dp", "ctx")
CHIPS = 64
MIB = 1024 * 1024
SCORE_FLOOR = -1e30
TOTAL_LIMIT = 2.0**90
EXP_SCALE = float(DH**-0.5 * np.log2(np.e))
WIDTHS = (1536, 1280, 1280)
OFFSETS = (0, 1536, 2816)
HALF = 4096

FLIPS = {
    "xa": (1, 0, 0),
    "xb": (3, 0, 0),
    "ya": (0, 1, 0),
    "yb": (0, 3, 0),
    "za": (0, 0, 1),
    "zb": (0, 0, 3),
}
SET_A = ("xa", "ya", "za")
SET_B = ("xb", "yb", "zb")


def rotate(names, by):
    return names[by:] + names[:by]


ORDERS = (
    tuple(rotate(SET_A, part) + SET_B for part in range(3)),
    tuple(rotate(SET_B, part) + SET_A for part in range(3)),
)


def place_of(index):
    dp, ctx = index // SLOTS, index % SLOTS
    y, z_hi, core = dp // 4, (dp // 2) % 2, dp % 2
    return ctx % 4, y, z_hi * 2 + ctx // 4, core


def index_of(x, y, z, core):
    return (y * 4 + (z // 2) * 2 + core) * SLOTS + (z % 2) * 4 + x


def flip_of(names):
    flips = [FLIPS[name] for name in names]
    return [functools.reduce(lambda a, b: a ^ b, axis) for axis in zip(*flips)]


def flip_pairs(names_of_core):
    pairs = []
    for index in range(2 * CHIPS):
        x, y, z, core = place_of(index)
        names = names_of_core[core]
        fx, fy, fz = flip_of((names,) if isinstance(names, str) else names)
        pairs.append((index, index_of(x ^ fx, y ^ fy, z ^ fz, core)))
    return pairs


def core_pairs(names_of_core=((), ())):
    pairs = []
    for index in range(2 * CHIPS):
        x, y, z, core = place_of(index)
        fx, fy, fz = flip_of(names_of_core[core]) if names_of_core[core] else (0, 0, 0)
        pairs.append((index, index_of(x ^ fx, y ^ fy, z ^ fz, 1 - core)))
    return pairs


def flip_table():
    table = np.zeros((2, CHIPS, 3), np.int32)
    for core in range(2):
        for block in range(CHIPS):
            for level, name in enumerate(ORDERS[core][0]):
                if (block >> (5 - level)) & 1:
                    table[core, block] ^= np.array(FLIPS[name], np.int32)
    return table


def dot(a, b, contract):
    return lax.dot_general(
        a, b, ((contract[:1], contract[1:]), ((), ())), preferred_element_type=jnp.float32
    )


def as_bf16(mask):
    return mask.astype(jnp.float32).astype(jnp.bfloat16)


def vmem_call(body, out_shape, scratch=(), smem=0, operands=(), mib=16, flops=0, nbytes=0):
    specs = [pl.BlockSpec(memory_space=pltpu.SMEM)] * smem
    specs += [pl.BlockSpec(memory_space=pltpu.VMEM)] * (len(operands) - smem)
    out_specs = jax.tree.map(lambda _: pl.BlockSpec(memory_space=pltpu.VMEM), out_shape)
    return pl.pallas_call(
        body,
        out_shape=out_shape,
        in_specs=specs,
        out_specs=out_specs,
        scratch_shapes=list(scratch),
        compiler_params=pltpu.CompilerParams(vmem_limit_bytes=mib * MIB),
        cost_estimate=pl.CostEstimate(flops=flops, bytes_accessed=nbytes, transcendentals=0),
    )(*operands)


def sort_kernel(dest_ref, rows_ref, sent_ref, held_ref, sorted_ref, sem_ref):
    rows_copy = pltpu.make_async_copy(rows_ref.at[0], held_ref, sem_ref.at[0])
    rows_copy.start()
    dest = dest_ref[...]
    target = dest >> 9
    slot = dest & (ROWS - 1)
    member = as_bf16(lax.broadcasted_iota(jnp.int32, (GROUPS, ROWS), 0) == target)
    same = dot(member, member, (0, 0))
    row = lax.broadcasted_iota(jnp.int32, (ROWS, ROWS), 0)
    col = lax.broadcasted_iota(jnp.int32, (ROWS, ROWS), 1)
    rank = jnp.sum(jnp.where(row < col, same, 0.0), axis=0, keepdims=True)
    place = target * (ROWS // GROUPS) + rank.astype(jnp.int32)
    order = as_bf16(row == place)
    line = lax.broadcasted_iota(jnp.int32, (DH, ROWS), 0)
    coded = jnp.where(line == 0, slot >> 4, jnp.where(line == 1, slot & 15, 0))
    coded = coded.astype(jnp.float32).astype(jnp.bfloat16)
    sorted_ref[:, 2 * DH : HEAD] = dot(order, coded, (1, 1)).astype(jnp.bfloat16)
    rows_copy.wait()
    sorted_ref[:, : 2 * DH] = dot(order, held_ref[:, QUERIES:], (1, 0)).astype(jnp.bfloat16)
    copies = []
    for at in range(2):
        if at > 0:
            cols = slice((at - 1) * QUERIES // 2, at * QUERIES // 2)
            sorted_ref[:, HEAD + cols.start : HEAD + cols.stop] = dot(
                order, held_ref[:, cols], (1, 0)
            ).astype(jnp.bfloat16)
        start, stop = (0, HEAD) if at == 0 else (HEAD, HEAD + QUERIES // 2)
        copies.append(
            pltpu.make_async_copy(
                sorted_ref.at[:, start:stop], sent_ref.at[:, start:stop], sem_ref.at[1 + at]
            )
        )
        copies[-1].start()
    cols = slice(QUERIES // 2, QUERIES)
    sorted_ref[:, HEAD + cols.start :] = dot(order, held_ref[:, cols], (1, 0)).astype(jnp.bfloat16)
    start = HEAD + cols.start
    copies.append(
        pltpu.make_async_copy(sorted_ref.at[:, start:], sent_ref.at[:, start:], sem_ref.at[3])
    )
    copies[-1].start()
    for copy in copies:
        copy.wait()


def place_kernel(got_ref, key_vals_ref, inverse_ref):
    lane = lax.broadcasted_iota(jnp.int32, (16, DH), 1)
    coef = jnp.where(lane == 0, 16.0, jnp.where(lane == 1, 1.0, 0.0)).astype(jnp.bfloat16)
    slots = dot(coef, got_ref[:, 2 * DH :], (1, 1))[:1].astype(jnp.int32)
    inverse = as_bf16(lax.broadcasted_iota(jnp.int32, (ROWS, ROWS), 0) == slots)
    inverse_ref[...] = inverse
    key_vals_ref[...] = dot(
        inverse, got_ref[:, : 2 * DH], (1, 0)
    ).astype(jnp.bfloat16)


def doc_starts(lengths_ref):
    start1 = lengths_ref[0, 0]
    start2 = start1 + lengths_ref[0, 1]
    start3 = start2 + lengths_ref[0, 2]

    def first_of(position):
        found = jnp.where(position >= start1, start1, 0)
        found = jnp.where(position >= start2, start2, found)
        return jnp.where(position >= start3, start3, found)

    return first_of


def visible_keys(first_of, p_first, k_first):
    q_pos = p_first + lax.broadcasted_iota(jnp.int32, (TILE, TILE), 0)
    k_pos = k_first + lax.broadcasted_iota(jnp.int32, (TILE, TILE), 1)
    return (k_pos >= first_of(q_pos)) & (k_pos <= q_pos)


def tile_weights(queries, keys, top, visible):
    scores = dot(queries, keys, (1, 1))
    if visible is not None:
        scores = jnp.where(visible, scores, SCORE_FLOOR)
    top = jnp.concatenate([top] * (scores.shape[1] // DH), axis=1)
    return jnp.exp2(scores * EXP_SCALE - top).astype(jnp.bfloat16)


def rows_of(h, tile=0):
    return slice((tile * HQ + h) * TILE, (tile * HQ + h + 1) * TILE)


def cols_of(h):
    return slice(h * DH, (h + 1) * DH)


def own_kernel(slot_ref, lengths_ref, inverse_ref, got_ref, kv_ref, q_ref, top_ref, acc_ref, v_ref):
    q_ref[...] = dot(inverse_ref[...], got_ref[:, HEAD:], (1, 0)).astype(jnp.bfloat16)
    v_ref[:, :DH] = kv_ref[:, DH:]
    v_ref[:, DH:] = jnp.ones((ROWS, DH), jnp.bfloat16)
    first_of = doc_starts(lengths_ref)
    ones = jnp.ones((DH, DH), jnp.bfloat16)
    for tile in range(ROWS // TILE):
        q_rows = slice(tile * TILE, (tile + 1) * TILE)
        p_first = slot_ref[0] * ROWS + tile * TILE
        own_keys = kv_ref[q_rows, :DH].astype(jnp.float32)
        for h in range(HQ):
            pair = q_ref[q_rows, cols_of(h)].astype(jnp.float32) * own_keys
            top_ref[rows_of(h, tile), :] = (
                dot(pair.astype(jnp.bfloat16), ones, (1, 0)) * EXP_SCALE
            )
        for at in range(tile, -1, -1):
            k_rows = slice(at * TILE, (at + 1) * TILE)
            visible = visible_keys(first_of, p_first, slot_ref[0] * ROWS + at * TILE)
            for h in range(HQ):
                weights = tile_weights(
                    q_ref[q_rows, cols_of(h)],
                    kv_ref[k_rows, :DH],
                    top_ref[rows_of(h, tile), :],
                    visible,
                )
                term = dot(weights, v_ref[k_rows, :], (1, 0))
                if at == tile:
                    acc_ref[rows_of(h, tile), :] = term
                else:
                    acc_ref[rows_of(h, tile), :] += term


def attend_kernel(
    slot_ref,
    lengths_ref,
    table_ref,
    q_ref,
    top_ref,
    total_ref,
    kv_ref,
    near0_ref,
    near1_ref,
    near2_ref,
    far0_ref,
    far1_ref,
    far2_ref,
    last_ref,
    *refs,
):
    grads, refs = refs[:6], refs[6:]
    (out_ref, own_ref, swap_ref), held, refs = refs[:3], refs[3:9], refs[9:]
    k_ref, v_ref, exact_ref, acc_ref, done_ref, sem_ref = refs
    copies = [
        pltpu.make_async_copy(grad_ref, held_ref, sem_ref.at[at])
        for at, (grad_ref, held_ref) in enumerate(zip(grads, held))
    ]
    for copy in copies:
        copy.start()
    slot = slot_ref[0]
    core = slot_ref[1]
    x = slot % 4
    k_ref[BACK * ROWS :, :] = kv_ref[:, :DH]
    v_ref[BACK * ROWS :, :DH] = kv_ref[:, DH:]
    v_ref[:, DH:] = jnp.ones(((BACK + 1) * ROWS, DH), jnp.bfloat16)
    came = (
        (near0_ref, (1, 0), (3, 0)),
        (near1_ref, (3, 0), (0, 1)),
        (near2_ref, (0, 1), (1, 0)),
        (far0_ref, (2, 0), (2, 0)),
        (far1_ref, (3, 1), (3, 1)),
        (far2_ref, (1, 1), (1, 1)),
        (last_ref, (2, 1), (2, 1)),
    )
    for came_ref, flip0, flip1 in came:
        flip_x = jnp.where(core == 0, flip0[0], flip1[0])
        flip_z = jnp.where(core == 0, flip0[1], flip1[1])
        back = slot - ((slot // 4) ^ flip_z) * 4 - (x ^ flip_x)

        @pl.when((back >= 1) & (back <= BACK))
        def _(came_ref=came_ref, back=back):
            at = pl.ds(pl.multiple_of((BACK - back) * ROWS, ROWS), ROWS)
            k_ref[at, :] = came_ref[:, :DH]
            v_ref[at, :DH] = came_ref[:, DH:]

    first_of = doc_starts(lengths_ref)
    for tile in range(ROWS // TILE):
        q_rows = slice(tile * TILE, (tile + 1) * TILE)
        p_first = slot * ROWS + tile * TILE
        low_first = first_of(p_first)
        high_first = first_of(p_first + TILE - 1)
        own_at = BACK * ROWS + tile * TILE
        count = (p_first - low_first + TILE - 1) // TILE
        clear = jnp.maximum(p_first - high_first, 0) // TILE
        acc_ref[...] = total_ref[tile * HQ * TILE : (tile + 1) * HQ * TILE, :]

        def add(j, masked, wide=1, tile=tile, q_rows=q_rows, p_first=p_first, own_at=own_at):
            at = pl.ds(pl.multiple_of(own_at - j * TILE, TILE), wide * TILE)
            visible = visible_keys(first_of, p_first, p_first - j * TILE) if masked else None
            for h in range(HQ):
                weights = tile_weights(
                    q_ref[q_rows, cols_of(h)], k_ref[at, :], top_ref[rows_of(h, tile), :], visible
                )
                acc_ref[rows_of(h), :] += dot(weights, v_ref[at, :], (1, 0))

        clear = jnp.maximum(clear, tile)

        fours = (clear - tile) // 4
        twos = (clear - tile - 4 * fours) // 2

        @pl.loop(0, fours)
        def _(i):
            add(4 + tile + 4 * i, False, 4)

        @pl.loop(0, twos)
        def _(i):
            add(2 + tile + 4 * fours + 2 * i, False, 2)

        @pl.loop(1 + tile + 4 * fours + 2 * twos, 1 + clear)
        def _(j):
            add(j, False)

        @pl.loop(1 + clear, 1 + count)
        def _(j):
            add(j, True)

        @pl.when(jnp.max(acc_ref[:, DH:]) > TOTAL_LIMIT)
        def _(q_rows=q_rows, p_first=p_first, own_at=own_at, count=count):
            exact_ref[...] = jnp.full_like(exact_ref, SCORE_FLOOR)
            acc_ref[...] = jnp.zeros_like(acc_ref)

            @pl.loop(0, 1 + count)
            def _(j):
                at = pl.ds(pl.multiple_of(own_at - j * TILE, TILE), TILE)
                visible = visible_keys(first_of, p_first, p_first - j * TILE)

                @pl.loop(0, HQ)
                def _(h):
                    rows = pl.ds(pl.multiple_of(h * TILE, TILE), TILE)
                    cols = pl.ds(pl.multiple_of(h * DH, DH), DH)
                    scores = dot(q_ref[q_rows, cols], k_ref[at, :], (1, 1))
                    scores = jnp.where(visible, scores, SCORE_FLOOR)
                    old = exact_ref[rows, :]
                    best = jnp.max(scores, axis=1, keepdims=True) * EXP_SCALE
                    top = jnp.maximum(old, best)
                    rescale = jnp.exp2(old - top)
                    exact_ref[rows, :] = top
                    weights = tile_weights(q_ref[q_rows, cols], k_ref[at, :], top, visible)
                    rescale = jnp.concatenate([rescale, rescale], axis=1)
                    acc_ref[rows, :] = acc_ref[rows, :] * rescale + dot(
                        weights, v_ref[at, :], (1, 0)
                    )

        for h in range(HQ):
            done = acc_ref[rows_of(h), :DH] / acc_ref[rows_of(h), DH:]
            out_ref[q_rows, cols_of(h)] = done.astype(jnp.bfloat16)
            done_ref[cols_of(h), q_rows] = done.T

    for side, ordered_ref in enumerate((own_ref, swap_ref)):

        @pl.loop(0, CHIPS, unroll=4)
        def _(block, side=side, ordered_ref=ordered_ref):
            at = pl.multiple_of(table_ref[side, block], 8)
            both = jnp.concatenate(
                [done_ref[pl.ds(at, 8), :], done_ref[pl.ds(at + 64, 8), :]], axis=0
            )
            ordered_ref[pl.ds(pl.multiple_of(block * 16, 16), 16), :] = both.astype(jnp.bfloat16)
    for copy in copies:
        copy.wait()


def project_kernel(level, half, left_ref, cols_ref, *refs):
    start_ref, out_ref = refs if len(refs) == 2 else (None, refs[0])
    run = 512 >> level
    step = min(run, 256)
    for at in range(0, 512, step):
        rows = slice(at, at + step)
        source = (at // run) * 2 * run + half * run + at % run
        term = dot(left_ref[source : source + step, :], cols_ref[...], (1, 0))
        if start_ref is not None:
            term += start_ref[rows, :]
        out_ref[rows, :] = term.astype(out_ref.dtype)


def shape(rows, cols, dtype=jnp.bfloat16):
    return jax.ShapeDtypeStruct((rows, cols), dtype)


def body(qkv_in, dest, lengths, grad_out):
    dp_at = lax.axis_index("dp")
    slot = lax.axis_index("ctx")
    core = dp_at % 2
    x, y, z = slot % 4, dp_at // 4, ((dp_at // 2) % 2) * 2 + slot // 4
    swap = core_pairs()

    tokens = grad_out[0]
    own_cols = [
        lax.dynamic_slice(tokens, (0, core * HALF + at), (ROWS, width))
        for at, width in zip(OFFSETS, WIDTHS)
    ]
    other_cols = [
        lax.ppermute(
            lax.dynamic_slice(tokens, (0, (1 - core) * HALF + at), (ROWS, width)), AXES, swap
        )
        for at, width in zip(OFFSETS, WIDTHS)
    ]

    sent = pl.pallas_call(
        sort_kernel,
        out_shape=shape(ROWS, SENT),
        in_specs=[
            pl.BlockSpec(memory_space=pltpu.VMEM),
            pl.BlockSpec(memory_space=pltpu.HBM),
        ],
        out_specs=pl.BlockSpec(memory_space=pltpu.HBM),
        scratch_shapes=[
            pltpu.VMEM((ROWS, QUERIES + 2 * DH), jnp.bfloat16),
            pltpu.VMEM((ROWS, SENT), jnp.bfloat16),
            pltpu.SemaphoreType.DMA((4,)),
        ],
        compiler_params=pltpu.CompilerParams(vmem_limit_bytes=60 * MIB),
        cost_estimate=pl.CostEstimate(flops=10**9, bytes_accessed=3 * MIB, transcendentals=0),
    )(dest, qkv_in)
    got = lax.all_to_all(
        sent.reshape(GROUPS, ROWS // GROUPS, SENT), "dp", 0, 0, tiled=True
    ).reshape(ROWS, SENT)
    key_vals, inverse = pl.pallas_call(
        place_kernel,
        grid=(1,),
        out_shape=(shape(ROWS, 2 * DH), shape(ROWS, ROWS)),
        in_specs=[pl.BlockSpec((ROWS, HEAD), lambda _: (0, 0))],
        out_specs=(
            pl.BlockSpec((ROWS, 2 * DH), lambda _: (0, 0)),
            pl.BlockSpec((ROWS, ROWS), lambda _: (0, 0)),
        ),
        compiler_params=pltpu.CompilerParams(vmem_limit_bytes=8 * MIB),
        cost_estimate=pl.CostEstimate(flops=2 * 10**8, bytes_accessed=MIB, transcendentals=0),
    )(got)
    near0 = lax.ppermute(key_vals, AXES, flip_pairs(("xa", "xb")))
    near1 = lax.ppermute(key_vals, AXES, flip_pairs(("xb", "za")))
    near2 = lax.ppermute(key_vals, AXES, flip_pairs(("za", "xa")))
    far0 = lax.ppermute(near0, AXES, flip_pairs(("xb", "xa")))
    far1 = lax.ppermute(near1, AXES, flip_pairs(("za", "xb")))
    far2 = lax.ppermute(near2, AXES, flip_pairs(("xa", "za")))
    last = lax.ppermute(far0, AXES, flip_pairs(("za", "za")))

    place = jnp.stack([slot, core]).astype(jnp.int32)
    queries, tops, totals = vmem_call(
        own_kernel,
        (
            shape(ROWS, QUERIES),
            shape(2 * HQ * TILE, DH, jnp.float32),
            shape(2 * HQ * TILE, 2 * DH, jnp.float32),
        ),
        scratch=(pltpu.VMEM((ROWS, 2 * DH), jnp.bfloat16),),
        smem=2,
        operands=(place, lengths, inverse, got, key_vals),
        mib=20,
        flops=2 * 10**9,
        nbytes=4 * MIB,
    )

    flips = jnp.asarray(flip_table())
    flips = jnp.where(core == 0, flips, flips[::-1])
    to_x, to_y, to_z = x ^ flips[..., 0], y ^ flips[..., 1], z ^ flips[..., 2]
    table = ((to_y * 2 + to_z // 2) * 128 + ((to_z % 2) * 4 + to_x) * 8).astype(jnp.int32)

    (table, queries, last), own_cols, other_cols = lax.optimization_barrier(
        ((table, queries, last), own_cols, other_cols)
    )
    vmem = pl.BlockSpec(memory_space=pltpu.VMEM)
    smem = pl.BlockSpec(memory_space=pltpu.SMEM)
    columns = (*own_cols, *other_cols)
    attention, left, swap_left, *columns = pl.pallas_call(
        attend_kernel,
        out_shape=(
            shape(ROWS, QUERIES),
            shape(QUERIES, ROWS),
            shape(QUERIES, ROWS),
            *(shape(*a.shape) for a in columns),
        ),
        in_specs=[smem] * 3 + [vmem] * 11 + [pl.BlockSpec(memory_space=pltpu.HBM)] * 6,
        out_specs=(vmem,) * 9,
        scratch_shapes=[
            pltpu.VMEM(((BACK + 1) * ROWS, DH), jnp.bfloat16),
            pltpu.VMEM(((BACK + 1) * ROWS, 2 * DH), jnp.bfloat16),
            pltpu.VMEM((HQ * TILE, DH), jnp.float32),
            pltpu.VMEM((HQ * TILE, 2 * DH), jnp.float32),
            pltpu.VMEM((QUERIES, ROWS), jnp.float32),
            pltpu.SemaphoreType.DMA((6,)),
        ],
        compiler_params=pltpu.CompilerParams(vmem_limit_bytes=20 * MIB),
        cost_estimate=pl.CostEstimate(
            flops=10**10, bytes_accessed=16 * MIB, transcendentals=0
        ),
    )(
        place,
        lengths,
        table,
        queries,
        tops,
        totals,
        key_vals,
        near0,
        near1,
        near2,
        far0,
        far1,
        far2,
        last,
        *columns,
    )
    own_cols, other_cols = columns[:3], columns[3:]
    left2 = lax.ppermute(swap_left, AXES, swap)

    def project(part, half, side, start, dtype):
        return vmem_call(
            functools.partial(project_kernel, part, half),
            shape(512, WIDTHS[part], dtype),
            operands=(side, *start),
            flops=2 * 512 * 512 * WIDTHS[part],
            nbytes=5 * MIB,
        )

    own_terms = [project(part, 1, left, (own_cols[part],), jnp.float32) for part in range(3)]
    sends = []
    for part in range(3):
        sends.append(project(part, 1, left2, (other_cols[part], own_terms[part]), jnp.bfloat16))
        left2, _ = lax.optimization_barrier((left2, sends[-1]))
    keeps = []
    for part in range(3):
        term = project(part, 0, left2, (other_cols[part],), jnp.float32)
        keeps.append(project(part, 0, left, (own_cols[part], term), jnp.bfloat16))
    coming = [
        lax.ppermute(sends[part], AXES, flip_pairs([ORDERS[c][part][0] for c in range(2)]))
        for part in range(3)
    ]
    keeps, coming[0] = lax.optimization_barrier((keeps, coming[0]))
    for level in range(3):
        for part in range(3):
            lead = 2 if (level, part) == (0, 1) else 1
            width = WIDTHS[part]
            came = coming[part]
            if True and part > 0:
                came, _ = lax.optimization_barrier((came, sends[part - 1]))
            halves = [
                [
                    a.reshape(lead, 2, -1, width)[:, bit].reshape(-1, width).astype(jnp.float32)
                    for a in (keeps[part], came)
                ]
                for bit in range(2)
            ]
            sends[part] = (halves[1][0] + halves[1][1]).astype(jnp.bfloat16)
            keeps[part] = halves[0][0] + halves[0][1]
            if level < 2:
                coming[part] = lax.ppermute(
                    sends[part],
                    AXES,
                    flip_pairs([ORDERS[c][part][level + 1] for c in range(2)]),
                )
    keep, send = jnp.concatenate(keeps, axis=1), jnp.concatenate(sends, axis=1)
    blocks = (
        (send[:32], (3,)),
        (keep[32:].astype(jnp.bfloat16), (4,)),
        (send[32:], (3, 4)),
    )
    coming = [
        lax.ppermute(
            block, AXES, flip_pairs([[ORDERS[c][0][level] for level in levels] for c in range(2)])
        )
        for block, levels in blocks
    ]
    coming = lax.optimization_barrier(coming)
    total = keep[:32]
    for came in coming:
        total = total + came.astype(jnp.float32)
    blocks = total.reshape(2, 2, 8, HALF)
    mine = lax.dynamic_index_in_dim(blocks, core, 1, keepdims=False)
    theirs = lax.dynamic_index_in_dim(blocks, 1 - core, 1, keepdims=False).astype(jnp.bfloat16)
    last_flip = [(ORDERS[c][0][5],) for c in range(2)]
    coming = [
        lax.ppermute(theirs[1], AXES, core_pairs(last_flip)),
        lax.ppermute(mine[1].astype(jnp.bfloat16), AXES, flip_pairs(last_flip)),
        lax.ppermute(theirs[0], AXES, swap),
    ]
    coming = [came.astype(jnp.float32) for came in lax.optimization_barrier(coming)]
    mine, came = mine[0] + coming[1], coming[0] + coming[2]
    grad_proj = jnp.where(
        core == 0,
        jnp.concatenate([mine, came], axis=1),
        jnp.concatenate([came, mine], axis=1),
    )
    return attention[None], grad_proj


def solution(mesh):
    in_specs = (P("dp", "ctx", None), P("dp", "ctx"), P("dp", None), P("dp", "ctx", None))
    out_specs = (P("dp", "ctx", None), P(("dp", "ctx"), None))
    return jax.shard_map(body, mesh=mesh, in_specs=in_specs, out_specs=out_specs, check_vma=False)
```

```python
import functools

import jax
import jax.numpy as jnp
import numpy as np
from jax import lax
from jax.experimental import pallas as pl
from jax.experimental.pallas import tpu as pltpu
from jax.sharding import PartitionSpec as P

HQ = 8
DH = 128
ROWS = 512
GROUPS = 16
SLOTS = 8
BACK = 4
QUERIES = HQ * DH
HEAD = 3 * DH
SENT = QUERIES + HEAD
TILE = 256
AXES = ("dp", "ctx")
CHIPS = 64
MIB = 1024 * 1024
SCORE_FLOOR = -1e30
TOTAL_LIMIT = 2.0**90
EXP_SCALE = float(DH**-0.5 * np.log2(np.e))
WIDTHS = (1536, 1408, 1152)
OFFSETS = (0, 1536, 2944)
HALF = 4096

FLIPS = {
    "xa": (1, 0, 0),
    "xb": (3, 0, 0),
    "ya": (0, 1, 0),
    "yb": (0, 3, 0),
    "za": (0, 0, 1),
    "zb": (0, 0, 3),
}
SET_A = ("xa", "ya", "za")
SET_B = ("xb", "yb", "zb")


def rotate(names, by):
    return names[by:] + names[:by]


ORDERS = (
    tuple(rotate(SET_A, part) + SET_B for part in range(3)),
    tuple(rotate(SET_B, part) + SET_A for part in range(3)),
)


def place_of(index):
    dp, ctx = index // SLOTS, index % SLOTS
    y, z_hi, core = dp // 4, (dp // 2) % 2, dp % 2
    return ctx % 4, y, z_hi * 2 + ctx // 4, core


def index_of(x, y, z, core):
    return (y * 4 + (z // 2) * 2 + core) * SLOTS + (z % 2) * 4 + x


def flip_of(names):
    flips = [FLIPS[name] for name in names]
    return [functools.reduce(lambda a, b: a ^ b, axis) for axis in zip(*flips)]


def flip_pairs(names_of_core):
    pairs = []
    for index in range(2 * CHIPS):
        x, y, z, core = place_of(index)
        names = names_of_core[core]
        fx, fy, fz = flip_of((names,) if isinstance(names, str) else names)
        pairs.append((index, index_of(x ^ fx, y ^ fy, z ^ fz, core)))
    return pairs


def core_pairs(names_of_core=((), ())):
    pairs = []
    for index in range(2 * CHIPS):
        x, y, z, core = place_of(index)
        fx, fy, fz = flip_of(names_of_core[core]) if names_of_core[core] else (0, 0, 0)
        pairs.append((index, index_of(x ^ fx, y ^ fy, z ^ fz, 1 - core)))
    return pairs


def flip_table():
    table = np.zeros((2, CHIPS, 3), np.int32)
    for core in range(2):
        for block in range(CHIPS):
            for level, name in enumerate(ORDERS[core][0]):
                if (block >> (5 - level)) & 1:
                    table[core, block] ^= np.array(FLIPS[name], np.int32)
    return table


def dot(a, b, contract):
    return lax.dot_general(
        a, b, ((contract[:1], contract[1:]), ((), ())), preferred_element_type=jnp.float32
    )


def as_bf16(mask):
    return mask.astype(jnp.float32).astype(jnp.bfloat16)


def vmem_call(body, out_shape, scratch=(), smem=0, operands=(), mib=16, flops=0, nbytes=0):
    specs = [pl.BlockSpec(memory_space=pltpu.SMEM)] * smem
    specs += [pl.BlockSpec(memory_space=pltpu.VMEM)] * (len(operands) - smem)
    out_specs = jax.tree.map(lambda _: pl.BlockSpec(memory_space=pltpu.VMEM), out_shape)
    return pl.pallas_call(
        body,
        out_shape=out_shape,
        in_specs=specs,
        out_specs=out_specs,
        scratch_shapes=list(scratch),
        compiler_params=pltpu.CompilerParams(vmem_limit_bytes=mib * MIB),
        cost_estimate=pl.CostEstimate(flops=flops, bytes_accessed=nbytes, transcendentals=0),
    )(*operands)


def sort_kernel(dest_ref, rows_ref, sent_ref, held_ref, sem_ref):
    rows_copy = pltpu.make_async_copy(rows_ref.at[0], held_ref, sem_ref)
    rows_copy.start()
    dest = dest_ref[...]
    target = dest >> 9
    slot = dest & (ROWS - 1)
    member = as_bf16(lax.broadcasted_iota(jnp.int32, (GROUPS, ROWS), 0) == target)
    same = dot(member, member, (0, 0))
    row = lax.broadcasted_iota(jnp.int32, (ROWS, ROWS), 0)
    col = lax.broadcasted_iota(jnp.int32, (ROWS, ROWS), 1)
    rank = jnp.sum(jnp.where(row < col, same, 0.0), axis=0, keepdims=True)
    place = target * (ROWS // GROUPS) + rank.astype(jnp.int32)
    order = as_bf16(row == place)
    line = lax.broadcasted_iota(jnp.int32, (DH, ROWS), 0)
    coded = jnp.where(line == 0, slot >> 4, jnp.where(line == 1, slot & 15, 0))
    coded = coded.astype(jnp.float32).astype(jnp.bfloat16)
    sent_ref[:, 2 * DH : HEAD] = dot(order, coded, (1, 1)).astype(jnp.bfloat16)
    rows_copy.wait()
    sent_ref[:, : 2 * DH] = dot(order, held_ref[:, QUERIES:], (1, 0)).astype(jnp.bfloat16)
    sent_ref[:, HEAD:] = dot(order, held_ref[:, :QUERIES], (1, 0)).astype(jnp.bfloat16)


def place_kernel(got_ref, key_vals_ref, inverse_ref):
    lane = lax.broadcasted_iota(jnp.int32, (16, DH), 1)
    coef = jnp.where(lane == 0, 16.0, jnp.where(lane == 1, 1.0, 0.0)).astype(jnp.bfloat16)
    slots = dot(coef, got_ref[:, 2 * DH :], (1, 1))[:1].astype(jnp.int32)
    inverse = as_bf16(lax.broadcasted_iota(jnp.int32, (ROWS, ROWS), 0) == slots)
    inverse_ref[...] = inverse
    key_vals_ref[...] = dot(
        inverse, got_ref[:, : 2 * DH], (1, 0)
    ).astype(jnp.bfloat16)


def doc_starts(lengths_ref):
    start1 = lengths_ref[0, 0]
    start2 = start1 + lengths_ref[0, 1]
    start3 = start2 + lengths_ref[0, 2]

    def first_of(position):
        found = jnp.where(position >= start1, start1, 0)
        found = jnp.where(position >= start2, start2, found)
        return jnp.where(position >= start3, start3, found)

    return first_of


def visible_keys(first_of, p_first, k_first):
    q_pos = p_first + lax.broadcasted_iota(jnp.int32, (TILE, TILE), 0)
    k_pos = k_first + lax.broadcasted_iota(jnp.int32, (TILE, TILE), 1)
    return (k_pos >= first_of(q_pos)) & (k_pos <= q_pos)


def tile_weights(queries, keys, top, visible):
    scores = dot(queries, keys, (1, 1))
    if visible is not None:
        scores = jnp.where(visible, scores, SCORE_FLOOR)
    top = jnp.concatenate([top] * (scores.shape[1] // DH), axis=1)
    return jnp.exp2(scores * EXP_SCALE - top).astype(jnp.bfloat16)


def rows_of(h, tile=0):
    return slice((tile * HQ + h) * TILE, (tile * HQ + h + 1) * TILE)


def cols_of(h):
    return slice(h * DH, (h + 1) * DH)


def own_kernel(slot_ref, lengths_ref, inverse_ref, got_ref, kv_ref, q_ref, top_ref, acc_ref, v_ref):
    q_ref[...] = dot(inverse_ref[...], got_ref[:, HEAD:], (1, 0)).astype(jnp.bfloat16)
    v_ref[:, :DH] = kv_ref[:, DH:]
    v_ref[:, DH:] = jnp.ones((ROWS, DH), jnp.bfloat16)
    first_of = doc_starts(lengths_ref)
    ones = jnp.ones((DH, DH), jnp.bfloat16)
    for tile in range(ROWS // TILE):
        q_rows = slice(tile * TILE, (tile + 1) * TILE)
        p_first = slot_ref[0] * ROWS + tile * TILE
        own_keys = kv_ref[q_rows, :DH].astype(jnp.float32)
        for h in range(HQ):
            pair = q_ref[q_rows, cols_of(h)].astype(jnp.float32) * own_keys
            top_ref[rows_of(h, tile), :] = (
                dot(pair.astype(jnp.bfloat16), ones, (1, 0)) * EXP_SCALE
            )
        for at in range(tile, -1, -1):
            k_rows = slice(at * TILE, (at + 1) * TILE)
            visible = visible_keys(first_of, p_first, slot_ref[0] * ROWS + at * TILE)
            for h in range(HQ):
                weights = tile_weights(
                    q_ref[q_rows, cols_of(h)],
                    kv_ref[k_rows, :DH],
                    top_ref[rows_of(h, tile), :],
                    visible,
                )
                term = dot(weights, v_ref[k_rows, :], (1, 0))
                if at == tile:
                    acc_ref[rows_of(h, tile), :] = term
                else:
                    acc_ref[rows_of(h, tile), :] += term


def attend_kernel(
    slot_ref,
    lengths_ref,
    table_ref,
    q_ref,
    top_ref,
    total_ref,
    kv_ref,
    near0_ref,
    near1_ref,
    near2_ref,
    far0_ref,
    far1_ref,
    far2_ref,
    last_ref,
    *refs,
):
    grads, refs = refs[:6], refs[6:]
    (out_ref, own_ref, swap_ref), held, refs = refs[:3], refs[3:9], refs[9:]
    k_ref, v_ref, exact_ref, acc_ref, done_ref, sem_ref = refs
    copies = [
        pltpu.make_async_copy(grad_ref, held_ref, sem_ref.at[at])
        for at, (grad_ref, held_ref) in enumerate(zip(grads, held))
    ]
    for copy in copies:
        copy.start()
    slot = slot_ref[0]
    core = slot_ref[1]
    x = slot % 4
    k_ref[BACK * ROWS :, :] = kv_ref[:, :DH]
    v_ref[BACK * ROWS :, :DH] = kv_ref[:, DH:]
    v_ref[:, DH:] = jnp.ones(((BACK + 1) * ROWS, DH), jnp.bfloat16)
    came = (
        (near0_ref, (1, 0), (3, 0)),
        (near1_ref, (3, 0), (0, 1)),
        (near2_ref, (0, 1), (1, 0)),
        (far0_ref, (2, 0), (2, 0)),
        (far1_ref, (3, 1), (3, 1)),
        (far2_ref, (1, 1), (1, 1)),
        (last_ref, (2, 1), (2, 1)),
    )
    for came_ref, flip0, flip1 in came:
        flip_x = jnp.where(core == 0, flip0[0], flip1[0])
        flip_z = jnp.where(core == 0, flip0[1], flip1[1])
        back = slot - ((slot // 4) ^ flip_z) * 4 - (x ^ flip_x)

        @pl.when((back >= 1) & (back <= BACK))
        def _(came_ref=came_ref, back=back):
            at = pl.ds(pl.multiple_of((BACK - back) * ROWS, ROWS), ROWS)
            k_ref[at, :] = came_ref[:, :DH]
            v_ref[at, :DH] = came_ref[:, DH:]

    first_of = doc_starts(lengths_ref)
    for tile in range(ROWS // TILE):
        q_rows = slice(tile * TILE, (tile + 1) * TILE)
        p_first = slot * ROWS + tile * TILE
        low_first = first_of(p_first)
        high_first = first_of(p_first + TILE - 1)
        own_at = BACK * ROWS + tile * TILE
        count = (p_first - low_first + TILE - 1) // TILE
        clear = jnp.maximum(p_first - high_first, 0) // TILE
        acc_ref[...] = total_ref[tile * HQ * TILE : (tile + 1) * HQ * TILE, :]

        def add(j, masked, wide=1, tile=tile, q_rows=q_rows, p_first=p_first, own_at=own_at):
            at = pl.ds(pl.multiple_of(own_at - j * TILE, TILE), wide * TILE)
            visible = visible_keys(first_of, p_first, p_first - j * TILE) if masked else None
            for h in range(HQ):
                weights = tile_weights(
                    q_ref[q_rows, cols_of(h)], k_ref[at, :], top_ref[rows_of(h, tile), :], visible
                )
                acc_ref[rows_of(h), :] += dot(weights, v_ref[at, :], (1, 0))

        clear = jnp.maximum(clear, tile)

        pairs = (clear - tile) // 2

        @pl.loop(0, pairs)
        def _(i):
            add(2 + tile + 2 * i, False, 2)

        @pl.loop(1 + tile + 2 * pairs, 1 + clear)
        def _(j):
            add(j, False)

        @pl.loop(1 + clear, 1 + count)
        def _(j):
            add(j, True)

        @pl.when(jnp.max(acc_ref[:, DH:]) > TOTAL_LIMIT)
        def _(q_rows=q_rows, p_first=p_first, own_at=own_at, count=count):
            exact_ref[...] = jnp.full_like(exact_ref, SCORE_FLOOR)
            acc_ref[...] = jnp.zeros_like(acc_ref)

            @pl.loop(0, 1 + count)
            def _(j):
                at = pl.ds(pl.multiple_of(own_at - j * TILE, TILE), TILE)
                visible = visible_keys(first_of, p_first, p_first - j * TILE)

                @pl.loop(0, HQ)
                def _(h):
                    rows = pl.ds(pl.multiple_of(h * TILE, TILE), TILE)
                    cols = pl.ds(pl.multiple_of(h * DH, DH), DH)
                    scores = dot(q_ref[q_rows, cols], k_ref[at, :], (1, 1))
                    scores = jnp.where(visible, scores, SCORE_FLOOR)
                    old = exact_ref[rows, :]
                    best = jnp.max(scores, axis=1, keepdims=True) * EXP_SCALE
                    top = jnp.maximum(old, best)
                    rescale = jnp.exp2(old - top)
                    exact_ref[rows, :] = top
                    weights = tile_weights(q_ref[q_rows, cols], k_ref[at, :], top, visible)
                    rescale = jnp.concatenate([rescale, rescale], axis=1)
                    acc_ref[rows, :] = acc_ref[rows, :] * rescale + dot(
                        weights, v_ref[at, :], (1, 0)
                    )

        for h in range(HQ):
            done = acc_ref[rows_of(h), :DH] / acc_ref[rows_of(h), DH:]
            out_ref[q_rows, cols_of(h)] = done.astype(jnp.bfloat16)
            done_ref[cols_of(h), q_rows] = done.T

    for side, ordered_ref in enumerate((own_ref, swap_ref)):

        @pl.loop(0, CHIPS, unroll=4)
        def _(block, side=side, ordered_ref=ordered_ref):
            at = pl.multiple_of(table_ref[side, block], 8)
            both = jnp.concatenate(
                [done_ref[pl.ds(at, 8), :], done_ref[pl.ds(at + 64, 8), :]], axis=0
            )
            ordered_ref[pl.ds(pl.multiple_of(block * 16, 16), 16), :] = both.astype(jnp.bfloat16)
    for copy in copies:
        copy.wait()


def project_kernel(level, half, left_ref, cols_ref, *refs):
    start_ref, out_ref = refs if len(refs) == 2 else (None, refs[0])
    run = 512 >> level
    step = min(run, 256)
    for at in range(0, 512, step):
        rows = slice(at, at + step)
        source = (at // run) * 2 * run + half * run + at % run
        term = dot(left_ref[source : source + step, :], cols_ref[...], (1, 0))
        if start_ref is not None:
            term += start_ref[rows, :]
        out_ref[rows, :] = term.astype(out_ref.dtype)


def shape(rows, cols, dtype=jnp.bfloat16):
    return jax.ShapeDtypeStruct((rows, cols), dtype)


def body(qkv_in, dest, lengths, grad_out):
    dp_at = lax.axis_index("dp")
    slot = lax.axis_index("ctx")
    core = dp_at % 2
    x, y, z = slot % 4, dp_at // 4, ((dp_at // 2) % 2) * 2 + slot // 4
    swap = core_pairs()

    tokens = grad_out[0]
    own_cols = [
        lax.dynamic_slice(tokens, (0, core * HALF + at), (ROWS, width))
        for at, width in zip(OFFSETS, WIDTHS)
    ]
    other_cols = [
        lax.ppermute(
            lax.dynamic_slice(tokens, (0, (1 - core) * HALF + at), (ROWS, width)), AXES, swap
        )
        for at, width in zip(OFFSETS, WIDTHS)
    ]

    sent = pl.pallas_call(
        sort_kernel,
        out_shape=shape(ROWS, SENT),
        in_specs=[
            pl.BlockSpec(memory_space=pltpu.VMEM),
            pl.BlockSpec(memory_space=pltpu.HBM),
        ],
        out_specs=pl.BlockSpec(memory_space=pltpu.VMEM),
        scratch_shapes=[
            pltpu.VMEM((ROWS, QUERIES + 2 * DH), jnp.bfloat16),
            pltpu.SemaphoreType.DMA,
        ],
        compiler_params=pltpu.CompilerParams(vmem_limit_bytes=60 * MIB),
        cost_estimate=pl.CostEstimate(flops=10**9, bytes_accessed=3 * MIB, transcendentals=0),
    )(dest, qkv_in)
    got = lax.all_to_all(
        sent.reshape(GROUPS, ROWS // GROUPS, SENT), "dp", 0, 0, tiled=True
    ).reshape(ROWS, SENT)
    key_vals, inverse = pl.pallas_call(
        place_kernel,
        grid=(1,),
        out_shape=(shape(ROWS, 2 * DH), shape(ROWS, ROWS)),
        in_specs=[pl.BlockSpec((ROWS, HEAD), lambda _: (0, 0))],
        out_specs=(
            pl.BlockSpec((ROWS, 2 * DH), lambda _: (0, 0)),
            pl.BlockSpec((ROWS, ROWS), lambda _: (0, 0)),
        ),
        compiler_params=pltpu.CompilerParams(vmem_limit_bytes=8 * MIB),
        cost_estimate=pl.CostEstimate(flops=2 * 10**8, bytes_accessed=MIB, transcendentals=0),
    )(got)
    near0 = lax.ppermute(key_vals, AXES, flip_pairs(("xa", "xb")))
    near1 = lax.ppermute(key_vals, AXES, flip_pairs(("xb", "za")))
    near2 = lax.ppermute(key_vals, AXES, flip_pairs(("za", "xa")))
    far0 = lax.ppermute(near0, AXES, flip_pairs(("xb", "xa")))
    far1 = lax.ppermute(near1, AXES, flip_pairs(("za", "xb")))
    far2 = lax.ppermute(near2, AXES, flip_pairs(("xa", "za")))
    last = lax.ppermute(far0, AXES, flip_pairs(("za", "za")))

    place = jnp.stack([slot, core]).astype(jnp.int32)
    queries, tops, totals = vmem_call(
        own_kernel,
        (
            shape(ROWS, QUERIES),
            shape(2 * HQ * TILE, DH, jnp.float32),
            shape(2 * HQ * TILE, 2 * DH, jnp.float32),
        ),
        scratch=(pltpu.VMEM((ROWS, 2 * DH), jnp.bfloat16),),
        smem=2,
        operands=(place, lengths, inverse, got, key_vals),
        mib=20,
        flops=2 * 10**9,
        nbytes=4 * MIB,
    )

    flips = jnp.asarray(flip_table())
    flips = jnp.where(core == 0, flips, flips[::-1])
    to_x, to_y, to_z = x ^ flips[..., 0], y ^ flips[..., 1], z ^ flips[..., 2]
    table = ((to_y * 2 + to_z // 2) * 128 + ((to_z % 2) * 4 + to_x) * 8).astype(jnp.int32)

    (table, queries, last), own_cols, other_cols = lax.optimization_barrier(
        ((table, queries, last), own_cols, other_cols)
    )
    vmem = pl.BlockSpec(memory_space=pltpu.VMEM)
    smem = pl.BlockSpec(memory_space=pltpu.SMEM)
    columns = (*own_cols, *other_cols)
    attention, left, swap_left, *columns = pl.pallas_call(
        attend_kernel,
        out_shape=(
            shape(ROWS, QUERIES),
            shape(QUERIES, ROWS),
            shape(QUERIES, ROWS),
            *(shape(*a.shape) for a in columns),
        ),
        in_specs=[smem] * 3 + [vmem] * 11 + [pl.BlockSpec(memory_space=pltpu.HBM)] * 6,
        out_specs=(vmem,) * 9,
        scratch_shapes=[
            pltpu.VMEM(((BACK + 1) * ROWS, DH), jnp.bfloat16),
            pltpu.VMEM(((BACK + 1) * ROWS, 2 * DH), jnp.bfloat16),
            pltpu.VMEM((HQ * TILE, DH), jnp.float32),
            pltpu.VMEM((HQ * TILE, 2 * DH), jnp.float32),
            pltpu.VMEM((QUERIES, ROWS), jnp.float32),
            pltpu.SemaphoreType.DMA((6,)),
        ],
        compiler_params=pltpu.CompilerParams(vmem_limit_bytes=20 * MIB),
        cost_estimate=pl.CostEstimate(
            flops=10**10, bytes_accessed=16 * MIB, transcendentals=0
        ),
    )(
        place,
        lengths,
        table,
        queries,
        tops,
        totals,
        key_vals,
        near0,
        near1,
        near2,
        far0,
        far1,
        far2,
        last,
        *columns,
    )
    own_cols, other_cols = columns[:3], columns[3:]
    left2 = lax.ppermute(swap_left, AXES, swap)

    def project(part, half, side, start, dtype):
        return vmem_call(
            functools.partial(project_kernel, part, half),
            shape(512, WIDTHS[part], dtype),
            operands=(side, *start),
            flops=2 * 512 * 512 * WIDTHS[part],
            nbytes=5 * MIB,
        )

    own_terms = [project(part, 1, left, (own_cols[part],), jnp.float32) for part in range(3)]
    sends = []
    for part in range(3):
        sends.append(project(part, 1, left2, (other_cols[part], own_terms[part]), jnp.bfloat16))
        left2, _ = lax.optimization_barrier((left2, sends[-1]))
    keeps = []
    for part in range(3):
        term = project(part, 0, left2, (other_cols[part],), jnp.float32)
        keeps.append(project(part, 0, left, (own_cols[part], term), jnp.bfloat16))
    coming = [
        lax.ppermute(sends[part], AXES, flip_pairs([ORDERS[c][part][0] for c in range(2)]))
        for part in range(3)
    ]
    keeps, coming[0] = lax.optimization_barrier((keeps, coming[0]))
    for level in range(3):
        for part in range(3):
            lead = 2 if (level, part) == (0, 1) else 1
            width = WIDTHS[part]
            came = coming[part]
            if True and part > 0:
                came, _ = lax.optimization_barrier((came, sends[part - 1]))
            halves = [
                [
                    a.reshape(lead, 2, -1, width)[:, bit].reshape(-1, width).astype(jnp.float32)
                    for a in (keeps[part], came)
                ]
                for bit in range(2)
            ]
            sends[part] = (halves[1][0] + halves[1][1]).astype(jnp.bfloat16)
            keeps[part] = halves[0][0] + halves[0][1]
            if level < 2:
                coming[part] = lax.ppermute(
                    sends[part],
                    AXES,
                    flip_pairs([ORDERS[c][part][level + 1] for c in range(2)]),
                )
    keep, send = jnp.concatenate(keeps, axis=1), jnp.concatenate(sends, axis=1)
    blocks = (
        (send[:32], (3,)),
        (keep[32:].astype(jnp.bfloat16), (4,)),
        (send[32:], (3, 4)),
    )
    coming = [
        lax.ppermute(
            block, AXES, flip_pairs([[ORDERS[c][0][level] for level in levels] for c in range(2)])
        )
        for block, levels in blocks
    ]
    coming = lax.optimization_barrier(coming)
    total = keep[:32]
    for came in coming:
        total = total + came.astype(jnp.float32)
    blocks = total.reshape(2, 2, 8, HALF)
    mine = lax.dynamic_index_in_dim(blocks, core, 1, keepdims=False)
    theirs = lax.dynamic_index_in_dim(blocks, 1 - core, 1, keepdims=False).astype(jnp.bfloat16)
    last_flip = [(ORDERS[c][0][5],) for c in range(2)]
    coming = [
        lax.ppermute(theirs[1], AXES, core_pairs(last_flip)),
        lax.ppermute(mine[1].astype(jnp.bfloat16), AXES, flip_pairs(last_flip)),
        lax.ppermute(theirs[0], AXES, swap),
    ]
    coming = [came.astype(jnp.float32) for came in lax.optimization_barrier(coming)]
    mine, came = mine[0] + coming[1], coming[0] + coming[2]
    grad_proj = jnp.where(
        core == 0,
        jnp.concatenate([mine, came], axis=1),
        jnp.concatenate([came, mine], axis=1),
    )
    return attention[None], grad_proj


def solution(mesh):
    in_specs = (P("dp", "ctx", None), P("dp", "ctx"), P("dp", None), P("dp", "ctx", None))
    out_specs = (P("dp", "ctx", None), P(("dp", "ctx"), None))
    return jax.shard_map(body, mesh=mesh, in_specs=in_specs, out_specs=out_specs, check_vma=False)
```

```python
import functools

import jax
import jax.numpy as jnp
import numpy as np
from jax import lax
from jax.experimental import pallas as pl
from jax.experimental.pallas import tpu as pltpu
from jax.sharding import PartitionSpec as P

HQ = 8
DH = 128
ROWS = 512
GROUPS = 16
SLOTS = 8
BACK = 4
QUERIES = HQ * DH
HEAD = 3 * DH
SENT = QUERIES + HEAD
TILE = 256
AXES = ("dp", "ctx")
CHIPS = 64
MIB = 1024 * 1024
SCORE_FLOOR = -1e30
TOTAL_LIMIT = 2.0**90
EXP_SCALE = float(DH**-0.5 * np.log2(np.e))
WIDTHS = (1536, 1280, 1280)
OFFSETS = (0, 1536, 2816)
HALF = 4096

FLIPS = {
    "xa": (1, 0, 0),
    "xb": (3, 0, 0),
    "ya": (0, 1, 0),
    "yb": (0, 3, 0),
    "za": (0, 0, 1),
    "zb": (0, 0, 3),
}
SET_A = ("xa", "ya", "za")
SET_B = ("xb", "yb", "zb")


def rotate(names, by):
    return names[by:] + names[:by]


ORDERS = (
    tuple(rotate(SET_A, part) + SET_B for part in range(3)),
    tuple(rotate(SET_B, part) + SET_A for part in range(3)),
)


def place_of(index):
    dp, ctx = index // SLOTS, index % SLOTS
    y, z_hi, core = dp // 4, (dp // 2) % 2, dp % 2
    return ctx % 4, y, z_hi * 2 + ctx // 4, core


def index_of(x, y, z, core):
    return (y * 4 + (z // 2) * 2 + core) * SLOTS + (z % 2) * 4 + x


def flip_of(names):
    flips = [FLIPS[name] for name in names]
    return [functools.reduce(lambda a, b: a ^ b, axis) for axis in zip(*flips)]


def flip_pairs(names_of_core):
    pairs = []
    for index in range(2 * CHIPS):
        x, y, z, core = place_of(index)
        names = names_of_core[core]
        fx, fy, fz = flip_of((names,) if isinstance(names, str) else names)
        pairs.append((index, index_of(x ^ fx, y ^ fy, z ^ fz, core)))
    return pairs


def core_pairs(names_of_core=((), ())):
    pairs = []
    for index in range(2 * CHIPS):
        x, y, z, core = place_of(index)
        fx, fy, fz = flip_of(names_of_core[core]) if names_of_core[core] else (0, 0, 0)
        pairs.append((index, index_of(x ^ fx, y ^ fy, z ^ fz, 1 - core)))
    return pairs


def flip_table():
    table = np.zeros((2, CHIPS, 3), np.int32)
    for core in range(2):
        for block in range(CHIPS):
            for level, name in enumerate(ORDERS[core][0]):
                if (block >> (5 - level)) & 1:
                    table[core, block] ^= np.array(FLIPS[name], np.int32)
    return table


def dot(a, b, contract):
    return lax.dot_general(
        a, b, ((contract[:1], contract[1:]), ((), ())), preferred_element_type=jnp.float32
    )


def as_bf16(mask):
    return mask.astype(jnp.float32).astype(jnp.bfloat16)


def vmem_call(body, out_shape, scratch=(), smem=0, operands=(), mib=16, flops=0, nbytes=0):
    specs = [pl.BlockSpec(memory_space=pltpu.SMEM)] * smem
    specs += [pl.BlockSpec(memory_space=pltpu.VMEM)] * (len(operands) - smem)
    out_specs = jax.tree.map(lambda _: pl.BlockSpec(memory_space=pltpu.VMEM), out_shape)
    return pl.pallas_call(
        body,
        out_shape=out_shape,
        in_specs=specs,
        out_specs=out_specs,
        scratch_shapes=list(scratch),
        compiler_params=pltpu.CompilerParams(vmem_limit_bytes=mib * MIB),
        cost_estimate=pl.CostEstimate(flops=flops, bytes_accessed=nbytes, transcendentals=0),
    )(*operands)


def sort_kernel(dest_ref, rows_ref, sent_ref, held_ref, sorted_ref, sem_ref):
    rows_copy = pltpu.make_async_copy(rows_ref.at[0], held_ref, sem_ref.at[0])
    rows_copy.start()
    dest = dest_ref[...]
    target = dest >> 9
    slot = dest & (ROWS - 1)
    member = as_bf16(lax.broadcasted_iota(jnp.int32, (GROUPS, ROWS), 0) == target)
    same = dot(member, member, (0, 0))
    row = lax.broadcasted_iota(jnp.int32, (ROWS, ROWS), 0)
    col = lax.broadcasted_iota(jnp.int32, (ROWS, ROWS), 1)
    rank = jnp.sum(jnp.where(row < col, same, 0.0), axis=0, keepdims=True)
    place = target * (ROWS // GROUPS) + rank.astype(jnp.int32)
    order = as_bf16(row == place)
    line = lax.broadcasted_iota(jnp.int32, (DH, ROWS), 0)
    coded = jnp.where(line == 0, slot >> 4, jnp.where(line == 1, slot & 15, 0))
    coded = coded.astype(jnp.float32).astype(jnp.bfloat16)
    sorted_ref[:, 2 * DH : HEAD] = dot(order, coded, (1, 1)).astype(jnp.bfloat16)
    rows_copy.wait()
    sorted_ref[:, : 2 * DH] = dot(order, held_ref[:, QUERIES:], (1, 0)).astype(jnp.bfloat16)
    copies = []
    for at in range(2):
        if at > 0:
            cols = slice((at - 1) * QUERIES // 2, at * QUERIES // 2)
            sorted_ref[:, HEAD + cols.start : HEAD + cols.stop] = dot(
                order, held_ref[:, cols], (1, 0)
            ).astype(jnp.bfloat16)
        start, stop = (0, HEAD) if at == 0 else (HEAD, HEAD + QUERIES // 2)
        copies.append(
            pltpu.make_async_copy(
                sorted_ref.at[:, start:stop], sent_ref.at[:, start:stop], sem_ref.at[1 + at]
            )
        )
        copies[-1].start()
    cols = slice(QUERIES // 2, QUERIES)
    sorted_ref[:, HEAD + cols.start :] = dot(order, held_ref[:, cols], (1, 0)).astype(jnp.bfloat16)
    start = HEAD + cols.start
    copies.append(
        pltpu.make_async_copy(sorted_ref.at[:, start:], sent_ref.at[:, start:], sem_ref.at[3])
    )
    copies[-1].start()
    for copy in copies:
        copy.wait()


def place_kernel(got_ref, key_vals_ref, inverse_ref):
    lane = lax.broadcasted_iota(jnp.int32, (16, DH), 1)
    coef = jnp.where(lane == 0, 16.0, jnp.where(lane == 1, 1.0, 0.0)).astype(jnp.bfloat16)
    slots = dot(coef, got_ref[:, 2 * DH :], (1, 1))[:1].astype(jnp.int32)
    inverse = as_bf16(lax.broadcasted_iota(jnp.int32, (ROWS, ROWS), 0) == slots)
    inverse_ref[...] = inverse
    key_vals_ref[...] = dot(
        inverse, got_ref[:, : 2 * DH], (1, 0)
    ).astype(jnp.bfloat16)


def doc_starts(lengths_ref):
    start1 = lengths_ref[0, 0]
    start2 = start1 + lengths_ref[0, 1]
    start3 = start2 + lengths_ref[0, 2]

    def first_of(position):
        found = jnp.where(position >= start1, start1, 0)
        found = jnp.where(position >= start2, start2, found)
        return jnp.where(position >= start3, start3, found)

    return first_of


def visible_keys(first_of, p_first, k_first):
    q_pos = p_first + lax.broadcasted_iota(jnp.int32, (TILE, TILE), 0)
    k_pos = k_first + lax.broadcasted_iota(jnp.int32, (TILE, TILE), 1)
    return (k_pos >= first_of(q_pos)) & (k_pos <= q_pos)


def tile_weights(queries, keys, top, visible):
    scores = dot(queries, keys, (1, 1))
    if visible is not None:
        scores = jnp.where(visible, scores, SCORE_FLOOR)
    top = jnp.concatenate([top] * (scores.shape[1] // DH), axis=1)
    return jnp.exp2(scores * EXP_SCALE - top).astype(jnp.bfloat16)


def rows_of(h, tile=0):
    return slice((tile * HQ + h) * TILE, (tile * HQ + h + 1) * TILE)


def cols_of(h):
    return slice(h * DH, (h + 1) * DH)


def own_kernel(slot_ref, lengths_ref, inverse_ref, got_ref, kv_ref, q_ref, top_ref, acc_ref, v_ref):
    q_ref[...] = dot(inverse_ref[...], got_ref[:, HEAD:], (1, 0)).astype(jnp.bfloat16)
    v_ref[:, :DH] = kv_ref[:, DH:]
    v_ref[:, DH:] = jnp.ones((ROWS, DH), jnp.bfloat16)
    first_of = doc_starts(lengths_ref)
    ones = jnp.ones((DH, DH), jnp.bfloat16)
    for tile in range(ROWS // TILE):
        q_rows = slice(tile * TILE, (tile + 1) * TILE)
        p_first = slot_ref[0] * ROWS + tile * TILE
        own_keys = kv_ref[q_rows, :DH].astype(jnp.float32)
        for h in range(HQ):
            pair = q_ref[q_rows, cols_of(h)].astype(jnp.float32) * own_keys
            top_ref[rows_of(h, tile), :] = (
                dot(pair.astype(jnp.bfloat16), ones, (1, 0)) * EXP_SCALE
            )
        for at in range(tile, -1, -1):
            k_rows = slice(at * TILE, (at + 1) * TILE)
            visible = visible_keys(first_of, p_first, slot_ref[0] * ROWS + at * TILE)
            for h in range(HQ):
                weights = tile_weights(
                    q_ref[q_rows, cols_of(h)],
                    kv_ref[k_rows, :DH],
                    top_ref[rows_of(h, tile), :],
                    visible,
                )
                term = dot(weights, v_ref[k_rows, :], (1, 0))
                if at == tile:
                    acc_ref[rows_of(h, tile), :] = term
                else:
                    acc_ref[rows_of(h, tile), :] += term


def attend_kernel(
    slot_ref,
    lengths_ref,
    table_ref,
    q_ref,
    top_ref,
    total_ref,
    kv_ref,
    near0_ref,
    near1_ref,
    near2_ref,
    far0_ref,
    far1_ref,
    far2_ref,
    last_ref,
    *refs,
):
    grads, refs = refs[:6], refs[6:]
    (out_ref, own_ref, swap_ref), held, refs = refs[:3], refs[3:9], refs[9:]
    k_ref, v_ref, exact_ref, acc_ref, done_ref, sem_ref = refs
    copies = [
        pltpu.make_async_copy(grad_ref, held_ref, sem_ref.at[at])
        for at, (grad_ref, held_ref) in enumerate(zip(grads, held))
    ]
    for copy in copies:
        copy.start()
    slot = slot_ref[0]
    core = slot_ref[1]
    x = slot % 4
    k_ref[BACK * ROWS :, :] = kv_ref[:, :DH]
    v_ref[BACK * ROWS :, :DH] = kv_ref[:, DH:]
    v_ref[:, DH:] = jnp.ones(((BACK + 1) * ROWS, DH), jnp.bfloat16)
    came = (
        (near0_ref, (1, 0), (3, 0)),
        (near1_ref, (3, 0), (0, 1)),
        (near2_ref, (0, 1), (1, 0)),
        (far0_ref, (2, 0), (2, 0)),
        (far1_ref, (3, 1), (3, 1)),
        (far2_ref, (1, 1), (1, 1)),
        (last_ref, (2, 1), (2, 1)),
    )
    for came_ref, flip0, flip1 in came:
        flip_x = jnp.where(core == 0, flip0[0], flip1[0])
        flip_z = jnp.where(core == 0, flip0[1], flip1[1])
        back = slot - ((slot // 4) ^ flip_z) * 4 - (x ^ flip_x)

        @pl.when((back >= 1) & (back <= BACK))
        def _(came_ref=came_ref, back=back):
            at = pl.ds(pl.multiple_of((BACK - back) * ROWS, ROWS), ROWS)
            k_ref[at, :] = came_ref[:, :DH]
            v_ref[at, :DH] = came_ref[:, DH:]

    first_of = doc_starts(lengths_ref)
    for tile in range(ROWS // TILE):
        q_rows = slice(tile * TILE, (tile + 1) * TILE)
        p_first = slot * ROWS + tile * TILE
        low_first = first_of(p_first)
        high_first = first_of(p_first + TILE - 1)
        own_at = BACK * ROWS + tile * TILE
        count = (p_first - low_first + TILE - 1) // TILE
        clear = jnp.maximum(p_first - high_first, 0) // TILE
        acc_ref[...] = total_ref[tile * HQ * TILE : (tile + 1) * HQ * TILE, :]

        def add(j, masked, wide=1, tile=tile, q_rows=q_rows, p_first=p_first, own_at=own_at):
            at = pl.ds(pl.multiple_of(own_at - j * TILE, TILE), wide * TILE)
            visible = visible_keys(first_of, p_first, p_first - j * TILE) if masked else None
            for h in range(HQ):
                weights = tile_weights(
                    q_ref[q_rows, cols_of(h)], k_ref[at, :], top_ref[rows_of(h, tile), :], visible
                )
                acc_ref[rows_of(h), :] += dot(weights, v_ref[at, :], (1, 0))

        clear = jnp.maximum(clear, tile)

        pairs = (clear - tile) // 2

        @pl.loop(0, pairs)
        def _(i):
            add(2 + tile + 2 * i, False, 2)

        @pl.loop(1 + tile + 2 * pairs, 1 + clear)
        def _(j):
            add(j, False)

        @pl.loop(1 + clear, 1 + count)
        def _(j):
            add(j, True)

        @pl.when(jnp.max(acc_ref[:, DH:]) > TOTAL_LIMIT)
        def _(q_rows=q_rows, p_first=p_first, own_at=own_at, count=count):
            exact_ref[...] = jnp.full_like(exact_ref, SCORE_FLOOR)
            acc_ref[...] = jnp.zeros_like(acc_ref)

            @pl.loop(0, 1 + count)
            def _(j):
                at = pl.ds(pl.multiple_of(own_at - j * TILE, TILE), TILE)
                visible = visible_keys(first_of, p_first, p_first - j * TILE)

                @pl.loop(0, HQ)
                def _(h):
                    rows = pl.ds(pl.multiple_of(h * TILE, TILE), TILE)
                    cols = pl.ds(pl.multiple_of(h * DH, DH), DH)
                    scores = dot(q_ref[q_rows, cols], k_ref[at, :], (1, 1))
                    scores = jnp.where(visible, scores, SCORE_FLOOR)
                    old = exact_ref[rows, :]
                    best = jnp.max(scores, axis=1, keepdims=True) * EXP_SCALE
                    top = jnp.maximum(old, best)
                    rescale = jnp.exp2(old - top)
                    exact_ref[rows, :] = top
                    weights = tile_weights(q_ref[q_rows, cols], k_ref[at, :], top, visible)
                    rescale = jnp.concatenate([rescale, rescale], axis=1)
                    acc_ref[rows, :] = acc_ref[rows, :] * rescale + dot(
                        weights, v_ref[at, :], (1, 0)
                    )

        for h in range(HQ):
            done = acc_ref[rows_of(h), :DH] / acc_ref[rows_of(h), DH:]
            out_ref[q_rows, cols_of(h)] = done.astype(jnp.bfloat16)
            done_ref[cols_of(h), q_rows] = done.T

    for side, ordered_ref in enumerate((own_ref, swap_ref)):

        @pl.loop(0, CHIPS, unroll=4)
        def _(block, side=side, ordered_ref=ordered_ref):
            at = pl.multiple_of(table_ref[side, block], 8)
            both = jnp.concatenate(
                [done_ref[pl.ds(at, 8), :], done_ref[pl.ds(at + 64, 8), :]], axis=0
            )
            ordered_ref[pl.ds(pl.multiple_of(block * 16, 16), 16), :] = both.astype(jnp.bfloat16)
    for copy in copies:
        copy.wait()


def project_kernel(level, half, left_ref, cols_ref, *refs):
    start_ref, out_ref = refs if len(refs) == 2 else (None, refs[0])
    run = 512 >> level
    step = min(run, 256)
    for at in range(0, 512, step):
        rows = slice(at, at + step)
        source = (at // run) * 2 * run + half * run + at % run
        term = dot(left_ref[source : source + step, :], cols_ref[...], (1, 0))
        if start_ref is not None:
            term += start_ref[rows, :]
        out_ref[rows, :] = term.astype(out_ref.dtype)


def shape(rows, cols, dtype=jnp.bfloat16):
    return jax.ShapeDtypeStruct((rows, cols), dtype)


def body(qkv_in, dest, lengths, grad_out):
    dp_at = lax.axis_index("dp")
    slot = lax.axis_index("ctx")
    core = dp_at % 2
    x, y, z = slot % 4, dp_at // 4, ((dp_at // 2) % 2) * 2 + slot // 4
    swap = core_pairs()

    tokens = grad_out[0]
    own_cols = [
        lax.dynamic_slice(tokens, (0, core * HALF + at), (ROWS, width))
        for at, width in zip(OFFSETS, WIDTHS)
    ]
    other_cols = [
        lax.ppermute(
            lax.dynamic_slice(tokens, (0, (1 - core) * HALF + at), (ROWS, width)), AXES, swap
        )
        for at, width in zip(OFFSETS, WIDTHS)
    ]

    sent = pl.pallas_call(
        sort_kernel,
        out_shape=shape(ROWS, SENT),
        in_specs=[
            pl.BlockSpec(memory_space=pltpu.VMEM),
            pl.BlockSpec(memory_space=pltpu.HBM),
        ],
        out_specs=pl.BlockSpec(memory_space=pltpu.HBM),
        scratch_shapes=[
            pltpu.VMEM((ROWS, QUERIES + 2 * DH), jnp.bfloat16),
            pltpu.VMEM((ROWS, SENT), jnp.bfloat16),
            pltpu.SemaphoreType.DMA((4,)),
        ],
        compiler_params=pltpu.CompilerParams(vmem_limit_bytes=60 * MIB),
        cost_estimate=pl.CostEstimate(flops=10**9, bytes_accessed=3 * MIB, transcendentals=0),
    )(dest, qkv_in)
    got = lax.all_to_all(
        sent.reshape(GROUPS, ROWS // GROUPS, SENT), "dp", 0, 0, tiled=True
    ).reshape(ROWS, SENT)
    key_vals, inverse = pl.pallas_call(
        place_kernel,
        grid=(1,),
        out_shape=(shape(ROWS, 2 * DH), shape(ROWS, ROWS)),
        in_specs=[pl.BlockSpec((ROWS, HEAD), lambda _: (0, 0))],
        out_specs=(
            pl.BlockSpec((ROWS, 2 * DH), lambda _: (0, 0)),
            pl.BlockSpec((ROWS, ROWS), lambda _: (0, 0)),
        ),
        compiler_params=pltpu.CompilerParams(vmem_limit_bytes=8 * MIB),
        cost_estimate=pl.CostEstimate(flops=2 * 10**8, bytes_accessed=MIB, transcendentals=0),
    )(got)
    near0 = lax.ppermute(key_vals, AXES, flip_pairs(("xa", "xb")))
    near1 = lax.ppermute(key_vals, AXES, flip_pairs(("xb", "za")))
    near2 = lax.ppermute(key_vals, AXES, flip_pairs(("za", "xa")))
    far0 = lax.ppermute(near0, AXES, flip_pairs(("xb", "xa")))
    far1 = lax.ppermute(near1, AXES, flip_pairs(("za", "xb")))
    far2 = lax.ppermute(near2, AXES, flip_pairs(("xa", "za")))
    last = lax.ppermute(far0, AXES, flip_pairs(("za", "za")))

    place = jnp.stack([slot, core]).astype(jnp.int32)
    queries, tops, totals = vmem_call(
        own_kernel,
        (
            shape(ROWS, QUERIES),
            shape(2 * HQ * TILE, DH, jnp.float32),
            shape(2 * HQ * TILE, 2 * DH, jnp.float32),
        ),
        scratch=(pltpu.VMEM((ROWS, 2 * DH), jnp.bfloat16),),
        smem=2,
        operands=(place, lengths, inverse, got, key_vals),
        mib=20,
        flops=2 * 10**9,
        nbytes=4 * MIB,
    )

    flips = jnp.asarray(flip_table())
    flips = jnp.where(core == 0, flips, flips[::-1])
    to_x, to_y, to_z = x ^ flips[..., 0], y ^ flips[..., 1], z ^ flips[..., 2]
    table = ((to_y * 2 + to_z // 2) * 128 + ((to_z % 2) * 4 + to_x) * 8).astype(jnp.int32)

    (table, queries, last), own_cols, other_cols = lax.optimization_barrier(
        ((table, queries, last), own_cols, other_cols)
    )
    vmem = pl.BlockSpec(memory_space=pltpu.VMEM)
    smem = pl.BlockSpec(memory_space=pltpu.SMEM)
    columns = (*own_cols, *other_cols)
    attention, left, swap_left, *columns = pl.pallas_call(
        attend_kernel,
        out_shape=(
            shape(ROWS, QUERIES),
            shape(QUERIES, ROWS),
            shape(QUERIES, ROWS),
            *(shape(*a.shape) for a in columns),
        ),
        in_specs=[smem] * 3 + [vmem] * 11 + [pl.BlockSpec(memory_space=pltpu.HBM)] * 6,
        out_specs=(vmem,) * 9,
        scratch_shapes=[
            pltpu.VMEM(((BACK + 1) * ROWS, DH), jnp.bfloat16),
            pltpu.VMEM(((BACK + 1) * ROWS, 2 * DH), jnp.bfloat16),
            pltpu.VMEM((HQ * TILE, DH), jnp.float32),
            pltpu.VMEM((HQ * TILE, 2 * DH), jnp.float32),
            pltpu.VMEM((QUERIES, ROWS), jnp.float32),
            pltpu.SemaphoreType.DMA((6,)),
        ],
        compiler_params=pltpu.CompilerParams(vmem_limit_bytes=20 * MIB),
        cost_estimate=pl.CostEstimate(
            flops=10**10, bytes_accessed=16 * MIB, transcendentals=0
        ),
    )(
        place,
        lengths,
        table,
        queries,
        tops,
        totals,
        key_vals,
        near0,
        near1,
        near2,
        far0,
        far1,
        far2,
        last,
        *columns,
    )
    own_cols, other_cols = columns[:3], columns[3:]
    left2 = lax.ppermute(swap_left, AXES, swap)

    def project(part, half, side, start, dtype):
        return vmem_call(
            functools.partial(project_kernel, part, half),
            shape(512, WIDTHS[part], dtype),
            operands=(side, *start),
            flops=2 * 512 * 512 * WIDTHS[part],
            nbytes=5 * MIB,
        )

    own_terms = [project(part, 1, left, (own_cols[part],), jnp.float32) for part in range(3)]
    sends = []
    for part in range(3):
        sends.append(project(part, 1, left2, (other_cols[part], own_terms[part]), jnp.bfloat16))
        left2, _ = lax.optimization_barrier((left2, sends[-1]))
    keeps = []
    for part in range(3):
        term = project(part, 0, left2, (other_cols[part],), jnp.float32)
        keeps.append(project(part, 0, left, (own_cols[part], term), jnp.bfloat16))
    coming = [
        lax.ppermute(sends[part], AXES, flip_pairs([ORDERS[c][part][0] for c in range(2)]))
        for part in range(3)
    ]
    keeps, coming[0] = lax.optimization_barrier((keeps, coming[0]))
    for level in range(3):
        for part in range(3):
            lead = 2 if (level, part) == (0, 1) else 1
            width = WIDTHS[part]
            came = coming[part]
            if True and part > 0:
                came, _ = lax.optimization_barrier((came, sends[part - 1]))
            halves = [
                [
                    a.reshape(lead, 2, -1, width)[:, bit].reshape(-1, width).astype(jnp.float32)
                    for a in (keeps[part], came)
                ]
                for bit in range(2)
            ]
            sends[part] = (halves[1][0] + halves[1][1]).astype(jnp.bfloat16)
            keeps[part] = halves[0][0] + halves[0][1]
            if level < 2:
                coming[part] = lax.ppermute(
                    sends[part],
                    AXES,
                    flip_pairs([ORDERS[c][part][level + 1] for c in range(2)]),
                )
    keep, send = jnp.concatenate(keeps, axis=1), jnp.concatenate(sends, axis=1)
    blocks = (
        (send[:32], (3,)),
        (keep[32:].astype(jnp.bfloat16), (4,)),
        (send[32:], (3, 4)),
    )
    coming = [
        lax.ppermute(
            block, AXES, flip_pairs([[ORDERS[c][0][level] for level in levels] for c in range(2)])
        )
        for block, levels in blocks
    ]
    coming = lax.optimization_barrier(coming)
    total = keep[:32]
    for came in coming:
        total = total + came.astype(jnp.float32)
    blocks = total.reshape(2, 2, 8, HALF)
    mine = lax.dynamic_index_in_dim(blocks, core, 1, keepdims=False)
    theirs = lax.dynamic_index_in_dim(blocks, 1 - core, 1, keepdims=False).astype(jnp.bfloat16)
    last_flip = [(ORDERS[c][0][5],) for c in range(2)]
    coming = [
        lax.ppermute(theirs[1], AXES, core_pairs(last_flip)),
        lax.ppermute(mine[1].astype(jnp.bfloat16), AXES, flip_pairs(last_flip)),
        lax.ppermute(theirs[0], AXES, swap),
    ]
    coming = [came.astype(jnp.float32) for came in lax.optimization_barrier(coming)]
    mine, came = mine[0] + coming[1], coming[0] + coming[2]
    grad_proj = jnp.where(
        core == 0,
        jnp.concatenate([mine, came], axis=1),
        jnp.concatenate([came, mine], axis=1),
    )
    return attention[None], grad_proj


def solution(mesh):
    in_specs = (P("dp", "ctx", None), P("dp", "ctx"), P("dp", None), P("dp", "ctx", None))
    out_specs = (P("dp", "ctx", None), P(("dp", "ctx"), None))
    return jax.shard_map(body, mesh=mesh, in_specs=in_specs, out_specs=out_specs, check_vma=False)
```
